32 devices in a mesh: rep: 4 (over z), node: 4 (over y, core), local: 2 (over x).
Axes of the slice: x: 2, y: 2, z: 4, core: 2. Of those that a mesh axis runs over, the one named last changes fastest.
Arguments:
- tokens: bfloat16 [2048, 7168], P(('rep', 'node', 'local')), parts along dimension 0, may hold values from -6 to 6
- expert_ids: int32 [2048, 8], P(('rep', 'node', 'local')), parts along dimension 0, may hold values from 0 to 31, as said below
- node_groups: int32 [2048, 2], P(('rep', 'node', 'local')), parts along dimension 0, may hold values from 0 to 3, as said below
- gate_levels: int32 [2048, 8], P(('rep', 'node', 'local')), parts along dimension 0, may hold values from 1 to 255
- expert_seeds: int32 [32], P(('node', 'local')), may hold values from 0 to 999999999
Outputs:
- routed_out: bfloat16 [2048, 7168], P(('rep', 'node', 'local')), parts along dimension 0
The draws below stay inside these ranges and needn't reach their ends.
There are 4 independent parts, one for each index of `rep`. The reference program is written for one: setup_inputs(seed, part) draws one part's arguments, and reference() takes and returns one part's arrays. A program takes and returns all parts, laid end to end along the dimension named above; an argument that names none is the same for every part. Nothing has to cross between parts.
Inputs may be any that keep to these rules, and one draw needn't show every extreme that they name: `expert_ids`: each row names 8 different experts; expert e belongs to node group e // 8. `node_groups`: each row names 2 different node groups.
All inputs are finite; a program needn't handle non-finite values.
Results may differ from the reference program's by a relative error of at most 0.0085.
Values may be sent and summed in bfloat16 or wider, within the bound.
A program may use at most 192 MiB of HBM per device.

```python
import math
import jax
import jax.numpy as jnp
from jax import lax

D = 7168
FF = 1024
TOP = 8
GROUP_PICK = 2
TOK_DEV = 64
GROUPS = 4
GROUP_EXPERTS = 8
EXPERTS = 32
TOKENS = 512
CAP = 16
N_NODE = 4
N_LOCAL = 2


def routing_draw(key):
    group_key = jax.random.fold_in(key, 101)
    hot_key = jax.random.fold_in(key, 202)
    score_key = jax.random.fold_in(key, 303)
    group_range = jnp.arange(GROUPS, dtype=jnp.int32)
    group_score = jax.random.randint(group_key, (TOKENS, GROUPS), 0, 1 << 20, dtype=jnp.int32) * GROUPS + group_range[None, :]
    unused_groups, chosen_groups = lax.top_k(group_score, GROUP_PICK)
    expert_range = jnp.arange(EXPERTS, dtype=jnp.int32)
    in_group = jnp.any((expert_range // GROUP_EXPERTS)[None, None, :] == chosen_groups[:, :, None], axis=1)
    hot_flag = jax.random.randint(hot_key, (EXPERTS,), 0, 6, dtype=jnp.int32) == 0
    base_score = jax.random.randint(score_key, (TOKENS, EXPERTS), 0, 1000, dtype=jnp.int32)
    expert_score = base_score + 150 * hot_flag.astype(jnp.int32)[None, :] + 600 * in_group.astype(jnp.int32)
    unused_values, chosen_experts = lax.top_k(expert_score * EXPERTS + expert_range[None, :], TOP)
    return (chosen_groups.astype(jnp.int32), chosen_experts.astype(jnp.int32))


def draw_node_groups(key, part):
    return routing_draw(key)[0]


def draw_expert_ids(key, part):
    return routing_draw(key)[1]


def with_ends(values, own_key, smallest, largest):
    index_at = [jax.random.randint(jax.random.fold_in(own_key, axis), (), 0, length) for axis, length in enumerate(values.shape)]
    longest = values.shape.index(max(values.shape))
    neighbour = index_at[:longest] + [(index_at[longest] + 1) % values.shape[longest]] + index_at[longest + 1:]
    return values.at[tuple(index_at)].set(smallest).at[tuple(neighbour)].set(largest)


def block_levels(rng, shape, shards, smallest, largest):
    def one(dim, blocks):
        draws = jax.random.uniform(jax.random.fold_in(jax.random.fold_in(rng, 6), dim), (blocks,), jnp.float32, smallest / len(shards), largest / len(shards))
        return jnp.repeat(jnp.exp(draws), shape[dim] // blocks).reshape((-1,) + (1,) * (len(shape) - dim - 1))

    factor_of = one(*shards[0])
    for cut in shards[1:]:
        factor_of = factor_of * one(*cut)
    return factor_of


def gaussian(rng, dims, spread, most, shards=(), held_as=jnp.bfloat16):
    factor_of = block_levels(rng, dims, shards, -0.22, 0.18) if shards else 1.0
    array = jax.random.normal(rng, dims, jnp.float32) * spread * factor_of
    return jnp.minimum(jnp.maximum(array, -most), most).astype(held_as)


def setup_inputs(seed: int = 0, part: int = 0) -> dict:
    keys = jax.random.split(jax.random.key(seed), 6)
    part_splits = jax.random.split(jax.random.fold_in(keys[5], part), 6)
    return {
        "tokens": gaussian(part_splits[0], (TOKENS, D), 1.0, 6.0, ((0, 8),)),
        "expert_ids": draw_expert_ids(jax.random.fold_in(jax.random.fold_in(keys[5], part), 71), part),
        "node_groups": draw_node_groups(jax.random.fold_in(jax.random.fold_in(keys[5], part), 71), part),
        "gate_levels": with_ends(jax.random.randint(part_splits[3], (TOKENS, TOP), 1, 256), jax.random.fold_in(part_splits[3], 1), 1, 255).astype(jnp.int32),
        "expert_seeds": with_ends(jax.random.randint(keys[4], (EXPERTS,), 0, 1000000000), jax.random.fold_in(keys[4], 1), 0, 999999999).astype(jnp.int32),
    }


route_scale = 2.5
salt_gate = 1013904223
salt_up = 1664525
salt_down = 22695477

def hashed_weight(expert_seed, salt_value, row_count, column_count, fan_in):
    row_index = lax.broadcasted_iota(jnp.int32, (row_count, column_count), 0)
    column_index = lax.broadcasted_iota(jnp.int32, (row_count, column_count), 1)
    hashed = (row_index * column_count + column_index) * 747796405 + expert_seed * 1103515245 + salt_value
    hashed = hashed ^ hashed >> 15
    hashed = hashed * 277803737
    hashed = hashed ^ hashed >> 13
    hashed = hashed * 668265263
    hashed = hashed ^ hashed >> 16
    sixteen_bits = (hashed >> 8 & 65535).astype(jnp.float32)
    return ((sixteen_bits - 32767.5) * (math.sqrt(3.0 / fan_in) / 32768.0)).astype(jnp.bfloat16)

def expert_block(block_rows, expert_seed):
    weight_gate = hashed_weight(expert_seed, salt_gate, D, FF, D)
    weight_up = hashed_weight(expert_seed, salt_up, D, FF, D)
    weight_down = hashed_weight(expert_seed, salt_down, FF, D, FF)
    gate_part = jnp.dot(block_rows, weight_gate, preferred_element_type=jnp.float32)
    up_part = jnp.dot(block_rows, weight_up, preferred_element_type=jnp.float32)
    hidden = (jax.nn.silu(gate_part) * up_part).astype(jnp.bfloat16)
    return jnp.dot(hidden, weight_down, preferred_element_type=jnp.float32).astype(jnp.bfloat16)

def group_mask(expert_ids, node_groups, group_size):
    return jnp.any((expert_ids // group_size)[:, :, None] == node_groups[:, None, :], axis=2)

def gate_of(gate_levels, in_group):
    levels = gate_levels.astype(jnp.float32)
    return route_scale * levels * in_group.astype(jnp.float32) / lax.optimization_barrier(jnp.sum(levels, axis=1, keepdims=True))

def rank_of(expert_ids, in_group, blocks, capacity, experts_total):
    expert_range = jnp.arange(experts_total, dtype=jnp.int32)
    hit_table = ((expert_ids[:, :, None] == expert_range[None, None, :]) & in_group[:, :, None]).astype(jnp.int32)
    present = lax.optimization_barrier(jnp.sum(hit_table, axis=1, dtype=jnp.int32))
    blocked = present.reshape(blocks, -1, experts_total)
    before = (jnp.cumsum(blocked, axis=1, dtype=jnp.int32) - blocked).reshape(-1, experts_total)
    slot_rank = lax.optimization_barrier(jnp.sum(hit_table * before[:, None, :], axis=2, dtype=jnp.int32)).astype(jnp.int32)
    kept_mask = in_group & (slot_rank < capacity)
    return (slot_rank, kept_mask)

def reference(tokens, expert_ids, node_groups, gate_levels, expert_seeds):
    sources = N_NODE * N_LOCAL
    in_group = group_mask(expert_ids, node_groups, GROUP_EXPERTS)
    gate_share = gate_of(gate_levels, in_group)
    slot_rank, kept_mask = rank_of(expert_ids, in_group, sources, CAP, EXPERTS)
    token_index = lax.broadcasted_iota(jnp.int32, (TOKENS, TOP), 0)
    source_index = token_index // TOK_DEV
    slot_total = EXPERTS * sources * CAP
    slot_index = jnp.where(kept_mask, (expert_ids * sources + source_index) * CAP + slot_rank, slot_total).astype(jnp.int32)
    slot_token = jnp.full((slot_total,), TOKENS, jnp.int32).at[slot_index.reshape(-1)].set(token_index.reshape(-1), mode='drop')
    slot_gate = jnp.zeros((slot_total,), jnp.float32).at[slot_index.reshape(-1)].set(gate_share.reshape(-1), mode='drop')
    padded = jnp.concatenate([tokens, jnp.zeros((1, D), tokens.dtype)], axis=0)

    def per_expert(running, scan_item):
        expert_seed, token_list, gate_list = scan_item
        outputs = expert_block(padded[token_list], expert_seed)
        running = running.at[token_list].add(gate_list[:, None] * outputs.astype(jnp.float32), mode='drop')
        return (running, None)
    summed, unused = lax.scan(per_expert, jnp.zeros((TOKENS, D), jnp.float32), (expert_seeds, slot_token.reshape(EXPERTS, -1), slot_gate.reshape(EXPERTS, -1)))
    return summed.astype(jnp.bfloat16)
```

```python
import functools
import math

import jax
import jax.numpy as jnp
from jax import lax
from jax.experimental import pallas as pl
from jax.experimental.pallas import tpu as pltpu
from jax.sharding import PartitionSpec as P

D = 7168
FF = 1024
TOP = 8
EXP_DEV = 4
AXES = ("node", "local")

route_scale = 2.5
salt_gate = 1013904223
salt_up = 1664525
salt_down = 22695477
INDEX_MUL = 747796405
SEED_MUL = 1103515245
SCALE_IN = math.sqrt(3.0 / D) / 32768.0
SCALE_OUT = math.sqrt(3.0 / FF) / 32768.0

ROWS = 512
COLS = 256
DOWN_COLS = 256
CHUNKS = 4


def as_int32(value):
    return jnp.int32((value + 2**31) % 2**32 - 2**31)


def centred(hashed):
    hashed = hashed ^ (hashed >> 15)
    hashed = hashed * jnp.int32(277803737)
    hashed = hashed ^ (hashed >> 13)
    hashed = hashed * jnp.int32(668265263)
    hashed = hashed ^ (hashed >> 16)
    sixteen = (hashed >> 8) & jnp.int32(65535)
    return (sixteen.astype(jnp.float32) - 32767.5).astype(jnp.bfloat16)


def fill_index(lin, columns):
    row = lax.broadcasted_iota(jnp.int32, lin.shape, 0)
    col = lax.broadcasted_iota(jnp.int32, lin.shape, 1)
    lin[...] = (row * columns + col) * as_int32(INDEX_MUL)


def offset(seed, salt, row, col, columns):
    return (row * columns + col) * as_int32(INDEX_MUL) + seed * as_int32(SEED_MUL) + jnp.int32(salt)


def make_kernel(seeds, gate_out, up_out, lin):
    tile = pl.program_id(0)

    @pl.when(tile == 0)
    def _():
        fill_index(lin, FF)

    @pl.loop(0, D // ROWS)
    def _(step):
        rows = pl.ds(pl.multiple_of(step * ROWS, ROWS), ROWS)
        for salt, out in ((salt_gate, gate_out), (salt_up, up_out)):
            out[rows, :] = centred(lin[...] + offset(seeds[0], salt, step * ROWS, tile * COLS, FF))


def make_weights(seeds):
    spec = pl.BlockSpec((D, COLS), lambda t: (0, t))
    return pl.pallas_call(
        make_kernel,
        grid=(FF // COLS,),
        in_specs=[pl.BlockSpec(memory_space=pltpu.SMEM)],
        out_specs=[spec, spec],
        out_shape=[jax.ShapeDtypeStruct((D, FF), jnp.bfloat16)] * 2,
        scratch_shapes=[pltpu.VMEM((ROWS, COLS), jnp.int32)],
        compiler_params=pltpu.CompilerParams(vmem_limit_bytes=48 << 20),
        cost_estimate=pl.CostEstimate(flops=2 * D * FF * 600, bytes_accessed=4 * D * FF, transcendentals=0),
    )(seeds)


def activation(gate_part, up_part, share):
    g = gate_part * SCALE_IN
    return (g / (1.0 + jnp.exp(-g)) * (up_part * SCALE_IN) * share).astype(jnp.bfloat16)


def up_kernel(seeds, x, share, act, lin, gate_acc, up_acc):
    expert = pl.program_id(0)
    tile = pl.program_id(1)

    @pl.when((expert == 0) & (tile == 0))
    def _():
        fill_index(lin, FF)

    gate_acc[...] = jnp.zeros_like(gate_acc)
    up_acc[...] = jnp.zeros_like(up_acc)
    seed = seeds[expert + 1]

    @pl.loop(0, D // ROWS)
    def _(step):
        x_part = x[0, :, pl.ds(pl.multiple_of(step * ROWS, ROWS), ROWS)]
        for salt, acc in ((salt_gate, gate_acc), (salt_up, up_acc)):
            w = centred(lin[...] + offset(seed, salt, step * ROWS, tile * COLS, FF))
            acc[...] += jnp.dot(x_part, w, preferred_element_type=jnp.float32)

    act[0] = activation(gate_acc[...], up_acc[...], share[0])


def run_up(seeds, x, share):
    experts, slots, width = x.shape
    return pl.pallas_call(
        up_kernel,
        grid=(experts, FF // COLS),
        in_specs=[
            pl.BlockSpec(memory_space=pltpu.SMEM),
            pl.BlockSpec((1, slots, width), lambda e, t: (e, 0, 0)),
            pl.BlockSpec((1, slots, 1), lambda e, t: (e, 0, 0)),
        ],
        out_specs=pl.BlockSpec((1, slots, COLS), lambda e, t: (e, 0, t)),
        out_shape=jax.ShapeDtypeStruct((experts, slots, FF), jnp.bfloat16),
        scratch_shapes=[
            pltpu.VMEM((ROWS, COLS), jnp.int32),
            pltpu.VMEM((slots, COLS), jnp.float32),
            pltpu.VMEM((slots, COLS), jnp.float32),
        ],
        compiler_params=pltpu.CompilerParams(vmem_limit_bytes=48 << 20),
        cost_estimate=pl.CostEstimate(
            flops=experts * 2 * D * FF * 600, bytes_accessed=2 * x.size, transcendentals=0
        ),
    )(seeds, x, share)


def down_kernel(first, seeds, act, place, out, lin, y):
    tile = pl.program_id(0)
    experts, slots, _ = act.shape

    @pl.when(tile == 0)
    def _():
        fill_index(lin, D)

    col = first + tile * DOWN_COLS

    @pl.loop(0, experts)
    def _(expert):
        seed = seeds[expert]
        total = jnp.zeros((slots, DOWN_COLS), jnp.float32)
        for step in range(FF // ROWS):
            w = centred(lin[...] + offset(seed, salt_down, step * ROWS, col, D))
            total += jnp.dot(
                act[expert, :, step * ROWS : (step + 1) * ROWS], w, preferred_element_type=jnp.float32
            )
        rows = pl.ds(pl.multiple_of(expert * slots, slots), slots)
        y[rows, :] = (total * SCALE_OUT).astype(jnp.bfloat16)

    out[...] = jnp.dot(place[...], y[...], preferred_element_type=jnp.float32).astype(jnp.bfloat16)


def run_down(seeds, act, place, first, columns):
    experts, slots, _ = act.shape
    tokens = place.shape[0]
    return pl.pallas_call(
        functools.partial(down_kernel, first),
        grid=(columns // DOWN_COLS,),
        in_specs=[
            pl.BlockSpec(memory_space=pltpu.SMEM),
            pl.BlockSpec(act.shape, lambda t: (0, 0, 0)),
            pl.BlockSpec(place.shape, lambda t: (0, 0)),
        ],
        out_specs=pl.BlockSpec((tokens, DOWN_COLS), lambda t: (0, t)),
        out_shape=jax.ShapeDtypeStruct((tokens, columns), jnp.bfloat16),
        scratch_shapes=[
            pltpu.VMEM((ROWS, DOWN_COLS), jnp.int32),
            pltpu.VMEM((experts * slots, DOWN_COLS), jnp.bfloat16),
        ],
        compiler_params=pltpu.CompilerParams(vmem_limit_bytes=48 << 20),
        cost_estimate=pl.CostEstimate(
            flops=experts * 2 * columns * FF * 600, bytes_accessed=2 * tokens * columns, transcendentals=0
        ),
    )(seeds, act, place)


def routing(meta, first_expert, group_size, capacity, tok_dev):
    total = meta.shape[0]
    sources = total // tok_dev
    ids, levels, groups = meta[:, :TOP], meta[:, TOP : 2 * TOP], meta[:, 2 * TOP :]
    in_group = jnp.any((ids // group_size)[:, :, None] == groups[:, None, :], axis=2)
    levels = levels.astype(jnp.float32)
    gate = (
        route_scale * levels * in_group.astype(jnp.float32) / jnp.sum(levels, axis=1, keepdims=True)
    )
    mine = first_expert + jnp.arange(EXP_DEV, dtype=jnp.int32)
    chosen = (ids[:, :, None] == mine) & in_group[:, :, None]
    hit = jnp.any(chosen, axis=1)
    share = jnp.sum(jnp.where(chosen, gate[:, :, None], 0.0), axis=1)
    earlier = jnp.tril(jnp.ones((tok_dev, tok_dev), jnp.bfloat16), -1)
    rank = jnp.einsum(
        "ts,bse->bte",
        earlier,
        hit.astype(jnp.bfloat16).reshape(sources, tok_dev, EXP_DEV),
        preferred_element_type=jnp.float32,
    ).reshape(total, EXP_DEV).astype(jnp.int32)
    source = (jnp.arange(total, dtype=jnp.int32) // tok_dev)[:, None]
    slot = jnp.where(hit & (rank < capacity), source * capacity + rank, -1)
    slots = jnp.arange(sources * capacity, dtype=jnp.int32)
    place = (slot[:, :, None] == slots).astype(jnp.bfloat16).reshape(total, -1)
    pick = slot.T[:, None, :] == slots[None, :, None]
    slot_share = jnp.sum(jnp.where(pick, share.T[:, None, :], 0.0), axis=2, keepdims=True)
    return pick.astype(jnp.bfloat16), place, slot_share


def on_device(tokens, expert_ids, node_groups, gate_levels, expert_seeds):
    tok_dev, width = tokens.shape
    devices_all = lax.axis_size(AXES)
    local_count = lax.axis_size("local")
    experts_total = EXP_DEV * devices_all
    capacity = max(2, tok_dev * TOP // experts_total)
    me = lax.axis_index("node") * local_count + lax.axis_index("local")

    meta = jnp.concatenate([expert_ids, gate_levels, node_groups], axis=1)
    meta = lax.all_gather(meta, AXES, axis=0, tiled=True)
    every = lax.all_gather(tokens, AXES, axis=0, tiled=True)
    pick, place, share = routing(meta, me * EXP_DEV, EXP_DEV * local_count, capacity, tok_dev)
    gate_w, up_w = make_weights(expert_seeds)

    slots = pick.shape[1]
    x = jnp.dot(
        pick.reshape(EXP_DEV * slots, -1), every, preferred_element_type=jnp.float32
    ).astype(jnp.bfloat16).reshape(EXP_DEV, slots, width)
    first_act = activation(
        jnp.dot(x[0], gate_w, preferred_element_type=jnp.float32),
        jnp.dot(x[0], up_w, preferred_element_type=jnp.float32),
        share[0],
    )
    act = jnp.concatenate([first_act[None], run_up(expert_seeds, x[1:], share[1:])], axis=0)

    columns = width // CHUNKS
    parts = []
    for chunk in range(CHUNKS):
        partial = run_down(expert_seeds, act, place, chunk * columns, columns)
        parts.append(lax.psum_scatter(partial, AXES, scatter_dimension=0, tiled=True))
    return jnp.concatenate(parts, axis=1)


def solution(mesh):
    rows = P(("rep", "node", "local"), None)
    return jax.shard_map(
        on_device,
        mesh=mesh,
        in_specs=(rows, rows, rows, rows, P(AXES)),
        out_specs=rows,
        check_vma=False,
    )
```

```python
import functools
import math

import jax
import jax.numpy as jnp
from jax import lax
from jax.experimental import pallas as pl
from jax.experimental.pallas import tpu as pltpu
from jax.sharding import PartitionSpec as P

D = 7168
FF = 1024
TOP = 8
EXP_DEV = 4
AXES = ("node", "local")

route_scale = 2.5
salt_gate = 1013904223
salt_up = 1664525
salt_down = 22695477
INDEX_MUL = 747796405
SEED_MUL = 1103515245
SCALE_IN = math.sqrt(3.0 / D) / 32768.0
SCALE_OUT = math.sqrt(3.0 / FF) / 32768.0

ROWS = 512
COLS = 256
DOWN_ROWS = 256
DOWN_COLS = 512
AHEAD = 2
META = 128


def as_int32(value):
    return jnp.int32((value + 2**31) % 2**32 - 2**31)


def centred(hashed):
    hashed = hashed ^ (hashed >> 15)
    hashed = hashed * jnp.int32(277803737)
    hashed = hashed ^ (hashed >> 13)
    hashed = hashed * jnp.int32(668265263)
    hashed = hashed ^ (hashed >> 16)
    sixteen = (hashed >> 8) & jnp.int32(65535)
    return (sixteen.astype(jnp.float32) - 32767.5).astype(jnp.bfloat16)


def fill_index(lin, columns):
    row = lax.broadcasted_iota(jnp.int32, lin.shape, 0)
    col = lax.broadcasted_iota(jnp.int32, lin.shape, 1)
    lin[...] = (row * columns + col) * as_int32(INDEX_MUL)


def offset(seed, salt, row, col, columns):
    return (row * columns + col) * as_int32(INDEX_MUL) + seed * as_int32(SEED_MUL) + jnp.int32(salt)


def make_kernel(seeds, gate_out, up_out, lin):
    expert = pl.program_id(0)
    tile = pl.program_id(1)

    @pl.when((expert == 0) & (tile == 0))
    def _():
        fill_index(lin, FF)

    seed = seeds[EXP_DEV - AHEAD + expert]

    @pl.loop(0, D // ROWS)
    def _(step):
        rows = pl.ds(pl.multiple_of(step * ROWS, ROWS), ROWS)
        for salt, out in ((salt_gate, gate_out), (salt_up, up_out)):
            out[0, rows, :] = centred(lin[...] + offset(seed, salt, step * ROWS, tile * COLS, FF))


def make_weights(seeds):
    spec = pl.BlockSpec((1, D, COLS), lambda e, t: (e, 0, t))
    return pl.pallas_call(
        make_kernel,
        grid=(AHEAD, FF // COLS),
        in_specs=[pl.BlockSpec(memory_space=pltpu.SMEM)],
        out_specs=[spec, spec],
        out_shape=[jax.ShapeDtypeStruct((AHEAD, D, FF), jnp.bfloat16)] * 2,
        scratch_shapes=[pltpu.VMEM((ROWS, COLS), jnp.int32)],
        compiler_params=pltpu.CompilerParams(vmem_limit_bytes=48 << 20),
        cost_estimate=pl.CostEstimate(
            flops=AHEAD * 2 * D * FF * 600, bytes_accessed=AHEAD * 4 * D * FF, transcendentals=0
        ),
    )(seeds)


def activation(gate_part, up_part, share):
    g = gate_part * SCALE_IN
    return (g / (1.0 + jnp.exp(-g)) * (up_part * SCALE_IN) * share).astype(jnp.bfloat16)


def up_kernel(seeds, x, share, gate_w, up_w, act, lin, acc):
    expert = pl.program_id(0)
    tile = pl.program_id(1)

    @pl.when((expert == 0) & (tile == 0))
    def _():
        fill_index(lin, FF)

    acc[...] = jnp.zeros_like(acc)
    seed = seeds[expert]

    @pl.loop(0, D // ROWS, unroll=2)
    def _(step):
        rows = pl.ds(pl.multiple_of(step * ROWS, ROWS), ROWS)
        hashed_x, ready_x = x[0, 0, :, rows], x[1, 0, :, rows]
        for which, (salt, ready) in enumerate(((salt_gate, gate_w), (salt_up, up_w))):
            w = centred(lin[...] + offset(seed, salt, step * ROWS, tile * COLS, FF))
            acc[2 + which] += jnp.dot(ready_x, ready[0, rows, :], preferred_element_type=jnp.float32)
            acc[which] += jnp.dot(hashed_x, w, preferred_element_type=jnp.float32)

    act[0, 0] = activation(acc[0], acc[1], share[0, 0])
    act[1, 0] = activation(acc[2], acc[3], share[1, 0])


def run_up(seeds, x, share, gate_w, up_w):
    experts, slots, _ = x.shape
    half = experts - AHEAD
    x = x.reshape(2, half, slots, -1)
    share = share.reshape(2, half, slots, 1)
    weights = pl.BlockSpec((1, D, COLS), lambda e, t: (e, 0, t))
    return pl.pallas_call(
        up_kernel,
        grid=(half, FF // COLS),
        in_specs=[
            pl.BlockSpec(memory_space=pltpu.SMEM),
            pl.BlockSpec((2, 1, slots, D), lambda e, t: (0, e, 0, 0)),
            pl.BlockSpec((2, 1, slots, 1), lambda e, t: (0, e, 0, 0)),
            weights,
            weights,
        ],
        out_specs=pl.BlockSpec((2, 1, slots, COLS), lambda e, t: (0, e, 0, t)),
        out_shape=jax.ShapeDtypeStruct((2, half, slots, FF), jnp.bfloat16),
        scratch_shapes=[
            pltpu.VMEM((ROWS, COLS), jnp.int32),
            pltpu.VMEM((4, slots, COLS), jnp.float32),
        ],
        compiler_params=pltpu.CompilerParams(vmem_limit_bytes=48 << 20),
        cost_estimate=pl.CostEstimate(
            flops=half * 2 * D * FF * 600, bytes_accessed=2 * x.size, transcendentals=0
        ),
    )(seeds, x, share, gate_w, up_w).reshape(experts, slots, FF)


def down_kernel(devices, local_count, seeds, act, place, out, lin, y, sent, arrived, send_sem, recv_sem):
    tile = pl.program_id(0)
    tiles = pl.num_programs(0)
    experts, slots, _ = act.shape
    tok_dev, width = out.shape
    me = lax.axis_index("node") * local_count + lax.axis_index("local")
    slot = lax.rem(tile, 2)

    def peer(step):
        return lax.rem(me + step, devices)

    def device(index):
        return {"node": index // local_count, "local": lax.rem(index, local_count)}

    barrier = pltpu.get_barrier_semaphore()

    @pl.when(tile == 0)
    def _():
        @pl.loop(1, devices)
        def _(step):
            pl.semaphore_signal(
                barrier, inc=1, device_id=device(peer(step)), device_id_type=pl.DeviceIdType.MESH
            )

        fill_index(lin, D)

    for expert in range(experts):
        total = jnp.zeros((slots, DOWN_COLS), jnp.float32)
        for step in range(FF // DOWN_ROWS):
            w = centred(
                lin[...] + offset(seeds[expert], salt_down, step * DOWN_ROWS, tile * DOWN_COLS, D)
            )
            total += jnp.dot(
                act[expert, :, step * DOWN_ROWS : (step + 1) * DOWN_ROWS],
                w,
                preferred_element_type=jnp.float32,
            )
        y[expert * slots : (expert + 1) * slots, :] = (total * SCALE_OUT).astype(jnp.bfloat16)

    def copy(step, where, column):
        to = peer(step)
        return pltpu.make_async_remote_copy(
            src_ref=sent.at[where, pl.ds(pl.multiple_of(to * tok_dev, tok_dev), tok_dev), :],
            dst_ref=arrived.at[me, :, pl.ds(pl.multiple_of(column * DOWN_COLS, DOWN_COLS), DOWN_COLS)],
            send_sem=send_sem.at[where, to],
            recv_sem=recv_sem.at[me],
            device_id=device(to),
            device_id_type=pl.DeviceIdType.MESH,
        )

    @pl.when(tile == 0)
    def _():
        pl.semaphore_wait(barrier, devices - 1)

    @pl.when(tile >= 2)
    def _():
        @pl.loop(1, devices)
        def _(step):
            copy(step, slot, tile - 2).wait_send()

    sent[slot] = jnp.dot(place[...], y[...], preferred_element_type=jnp.float32).astype(jnp.bfloat16)

    @pl.loop(1, devices)
    def _(step):
        copy(step, slot, tile).start()

    own = pl.ds(pl.multiple_of(me * tok_dev, tok_dev), tok_dev)
    columns = pl.ds(pl.multiple_of(tile * DOWN_COLS, DOWN_COLS), DOWN_COLS)
    arrived[me, :, columns] = sent[slot, own, :]

    @pl.when(tile == tiles - 1)
    def _():
        @pl.loop(1, devices)
        def _(step):
            copy(step, 1 - slot, tile - 1).wait_send()
            copy(step, slot, tile).wait_send()
            source = peer(step)
            pltpu.make_async_remote_copy(
                src_ref=arrived.at[source],
                dst_ref=arrived.at[source],
                send_sem=send_sem.at[0, source],
                recv_sem=recv_sem.at[source],
                device_id=device(source),
                device_id_type=pl.DeviceIdType.MESH,
            ).wait_recv()

        @pl.loop(0, width // DOWN_COLS)
        def _(part):
            span = pl.ds(pl.multiple_of(part * DOWN_COLS, DOWN_COLS), DOWN_COLS)

            def add(source, total):
                return total + arrived[source, :, span].astype(jnp.float32)

            total = lax.fori_loop(0, devices, add, jnp.zeros((tok_dev, DOWN_COLS), jnp.float32))
            out[:, span] = total.astype(jnp.bfloat16)


def run_down(seeds, act, place, tok_dev, width, devices, local_count):
    experts, slots, _ = act.shape
    tokens = place.shape[0]
    return pl.pallas_call(
        functools.partial(down_kernel, devices, local_count),
        grid=(width // DOWN_COLS,),
        in_specs=[
            pl.BlockSpec(memory_space=pltpu.SMEM),
            pl.BlockSpec(act.shape, lambda t: (0, 0, 0)),
            pl.BlockSpec(place.shape, lambda t: (0, 0)),
        ],
        out_specs=pl.BlockSpec((tok_dev, width), lambda t: (0, 0)),
        out_shape=jax.ShapeDtypeStruct((tok_dev, width), jnp.bfloat16),
        scratch_shapes=[
            pltpu.VMEM((DOWN_ROWS, DOWN_COLS), jnp.int32),
            pltpu.VMEM((experts * slots, DOWN_COLS), jnp.bfloat16),
            pltpu.VMEM((2, tokens, DOWN_COLS), jnp.bfloat16),
            pltpu.VMEM((devices, tok_dev, width), jnp.bfloat16),
            pltpu.SemaphoreType.DMA((2, devices)),
            pltpu.SemaphoreType.DMA((devices,)),
        ],
        compiler_params=pltpu.CompilerParams(
            vmem_limit_bytes=56 << 20, collective_id=0, has_side_effects=True
        ),
        cost_estimate=pl.CostEstimate(
            flops=experts * 2 * width * FF * 600, bytes_accessed=2 * tokens * width, transcendentals=0
        ),
    )(seeds, act, place)


def routing(meta, first_expert, group_size, capacity, tok_dev):
    total = meta.shape[0]
    sources = total // tok_dev
    ids, levels, groups = meta[:, :TOP], meta[:, TOP : 2 * TOP], meta[:, 2 * TOP :]
    in_group = jnp.any((ids // group_size)[:, :, None] == groups[:, None, :], axis=2)
    levels = levels.astype(jnp.float32)
    gate = (
        route_scale * levels * in_group.astype(jnp.float32) / jnp.sum(levels, axis=1, keepdims=True)
    )
    mine = first_expert + jnp.arange(EXP_DEV, dtype=jnp.int32)
    chosen = (ids[:, :, None] == mine) & in_group[:, :, None]
    hit = jnp.any(chosen, axis=1)
    share = jnp.sum(jnp.where(chosen, gate[:, :, None], 0.0), axis=1)
    earlier = jnp.tril(jnp.ones((tok_dev, tok_dev), jnp.bfloat16), -1)
    rank = jnp.einsum(
        "ts,bse->bte",
        earlier,
        hit.astype(jnp.bfloat16).reshape(sources, tok_dev, EXP_DEV),
        preferred_element_type=jnp.float32,
    ).reshape(total, EXP_DEV).astype(jnp.int32)
    source = (jnp.arange(total, dtype=jnp.int32) // tok_dev)[:, None]
    slot = jnp.where(hit & (rank < capacity), source * capacity + rank, -1)
    slots = jnp.arange(sources * capacity, dtype=jnp.int32)
    place = (slot[:, :, None] == slots).astype(jnp.bfloat16).reshape(total, -1)
    pick = slot.T[:, None, :] == slots[None, :, None]
    slot_share = jnp.sum(jnp.where(pick, share.T[:, None, :], 0.0), axis=2, keepdims=True)
    return pick.astype(jnp.bfloat16), place, slot_share


def on_device(tokens, expert_ids, node_groups, gate_levels, expert_seeds):
    tok_dev, width = tokens.shape
    devices_all = lax.axis_size(AXES)
    local_count = lax.axis_size("local")
    experts_total = EXP_DEV * devices_all
    capacity = max(2, tok_dev * TOP // experts_total)
    me = lax.axis_index("node") * local_count + lax.axis_index("local")

    meta = jnp.concatenate([expert_ids, gate_levels, node_groups], axis=1).astype(jnp.bfloat16)
    meta = jnp.pad(meta, ((0, 0), (0, META - meta.shape[1])))
    every = lax.all_gather(jnp.concatenate([tokens, meta], axis=1), AXES, axis=0, tiled=True)
    gate_w, up_w = make_weights(expert_seeds)
    pick, place, share = routing(
        every[:, width : width + 2 * TOP + node_groups.shape[1]].astype(jnp.int32),
        me * EXP_DEV,
        EXP_DEV * local_count,
        capacity,
        tok_dev,
    )

    slots = pick.shape[1]
    x = jnp.dot(
        pick.reshape(EXP_DEV * slots, -1), every, preferred_element_type=jnp.float32
    ).astype(jnp.bfloat16).reshape(EXP_DEV, slots, -1)
    act = run_up(expert_seeds, x, share, gate_w, up_w)
    return run_down(expert_seeds, act, place, tok_dev, width, devices_all, local_count)


def solution(mesh):
    rows = P(("rep", "node", "local"), None)
    return jax.shard_map(
        on_device,
        mesh=mesh,
        in_specs=(rows, rows, rows, rows, P(AXES)),
        out_specs=rows,
        check_vma=False,
    )
```

```python
import functools
import math

import jax
import jax.numpy as jnp
from jax import lax
from jax.experimental import pallas as pl
from jax.experimental.pallas import tpu as pltpu
from jax.sharding import PartitionSpec as P

D = 7168
FF = 1024
TOP = 8
EXP_DEV = 4
AXES = ("node", "local")

route_scale = 2.5
salt_gate = 1013904223
salt_up = 1664525
salt_down = 22695477
INDEX_MUL = 747796405
SEED_MUL = 1103515245
SCALE_IN = math.sqrt(3.0 / D) / 8388608.0
SCALE_OUT = math.sqrt(3.0 / FF) / 8388608.0

ROWS = 512
COLS = 256
PIECE = 64
DOWN_COLS = 512
AHEAD = 2
META = 128


def as_int32(value):
    return jnp.int32((value + 2**31) % 2**32 - 2**31)


def centred(hashed):
    hashed = hashed ^ (hashed >> 15)
    hashed = hashed * jnp.int32(277803737)
    hashed = hashed ^ (hashed >> 13)
    hashed = hashed * jnp.int32(668265263)
    hashed = hashed ^ (hashed >> 16)
    sixteen = (hashed & jnp.int32(65535 << 8)).astype(jnp.float32)
    return (sixteen - 32767.5 * 256.0).astype(jnp.bfloat16)


def fill_index(lin, columns):
    row = lax.broadcasted_iota(jnp.int32, lin.shape, 0)
    col = lax.broadcasted_iota(jnp.int32, lin.shape, 1)
    lin[...] = (row * columns + col) * as_int32(INDEX_MUL)


def hash_rows(out, where, lin, base, rows, columns):
    for piece in range(0, rows, PIECE):
        start = base + as_int32(piece * columns * INDEX_MUL)
        out[(*where, slice(piece, piece + PIECE), slice(None))] = centred(lin[...] + start)


def offset(seed, salt, row, col, columns):
    return (row * columns + col) * as_int32(INDEX_MUL) + seed * as_int32(SEED_MUL) + jnp.int32(salt)


def make_kernel(seeds, gate_out, up_out, lin):
    expert = pl.program_id(0)
    tile = pl.program_id(1)

    @pl.when((expert == 0) & (tile == 0))
    def _():
        fill_index(lin, FF)

    seed = seeds[EXP_DEV - AHEAD + expert]

    @pl.loop(0, D // ROWS)
    def _(step):
        rows = pl.ds(pl.multiple_of(step * ROWS, ROWS), ROWS)
        for salt, out in ((salt_gate, gate_out), (salt_up, up_out)):
            base = offset(seed, salt, step * ROWS, tile * COLS, FF)
            hash_rows(out.at[0, rows, :], (), lin, base, ROWS, FF)


def make_weights(seeds):
    spec = pl.BlockSpec((1, D, COLS), lambda e, t: (e, 0, t))
    return pl.pallas_call(
        make_kernel,
        grid=(AHEAD, FF // COLS),
        in_specs=[pl.BlockSpec(memory_space=pltpu.SMEM)],
        out_specs=[spec, spec],
        out_shape=[jax.ShapeDtypeStruct((AHEAD, D, FF), jnp.bfloat16)] * 2,
        scratch_shapes=[pltpu.VMEM((PIECE, COLS), jnp.int32)],
        compiler_params=pltpu.CompilerParams(vmem_limit_bytes=48 << 20),
        cost_estimate=pl.CostEstimate(
            flops=AHEAD * 2 * D * FF * 600, bytes_accessed=AHEAD * 4 * D * FF, transcendentals=0
        ),
    )(seeds)


def activation(gate_part, up_part, share):
    g = gate_part * SCALE_IN
    return (g / (1.0 + jnp.exp(-g)) * (up_part * SCALE_IN) * share).astype(jnp.bfloat16)


def up_kernel(seeds, x, share, gate_w, up_w, act, lin, made, acc):
    expert = pl.program_id(0)
    tile = pl.program_id(1)

    @pl.when((expert == 0) & (tile == 0))
    def _():
        fill_index(lin, FF)

    acc[...] = jnp.zeros_like(acc)
    seed = seeds[expert]

    def make(step, slot):
        for which, salt in enumerate((salt_gate, salt_up)):
            base = offset(seed, salt, step * ROWS, tile * COLS, FF)
            hash_rows(made, (slot, which), lin, base, ROWS, FF)

    def use(step, slot):
        rows = pl.ds(pl.multiple_of(step * ROWS, ROWS), ROWS)
        hashed_x, ready_x = x[0, 0, :, rows], x[1, 0, :, rows]
        for which, ready in enumerate((gate_w, up_w)):
            acc[2 + which] += jnp.dot(ready_x, ready[0, rows, :], preferred_element_type=jnp.float32)
            acc[which] += jnp.dot(hashed_x, made[slot, which], preferred_element_type=jnp.float32)

    steps = D // ROWS
    make(0, 0)

    @pl.loop(0, steps // 2 - 1)
    def _(pair):
        make(2 * pair + 1, 1)
        use(2 * pair, 0)
        make(2 * pair + 2, 0)
        use(2 * pair + 1, 1)

    make(steps - 1, 1)
    use(steps - 2, 0)
    use(steps - 1, 1)

    act[0, 0] = activation(acc[0], acc[1], share[0, 0])
    act[1, 0] = activation(acc[2], acc[3], share[1, 0])


def run_up(seeds, x, share, gate_w, up_w):
    experts, slots, _ = x.shape
    half = experts - AHEAD
    x = x.reshape(2, half, slots, -1)
    share = share.reshape(2, half, slots, 1)
    weights = pl.BlockSpec((1, D, COLS), lambda e, t: (e, 0, t))
    return pl.pallas_call(
        up_kernel,
        grid=(half, FF // COLS),
        in_specs=[
            pl.BlockSpec(memory_space=pltpu.SMEM),
            pl.BlockSpec((2, 1, slots, D), lambda e, t: (0, e, 0, 0)),
            pl.BlockSpec((2, 1, slots, 1), lambda e, t: (0, e, 0, 0)),
            weights,
            weights,
        ],
        out_specs=pl.BlockSpec((2, 1, slots, COLS), lambda e, t: (0, e, 0, t)),
        out_shape=jax.ShapeDtypeStruct((2, half, slots, FF), jnp.bfloat16),
        scratch_shapes=[
            pltpu.VMEM((PIECE, COLS), jnp.int32),
            pltpu.VMEM((2, 2, ROWS, COLS), jnp.bfloat16),
            pltpu.VMEM((4, slots, COLS), jnp.float32),
        ],
        compiler_params=pltpu.CompilerParams(vmem_limit_bytes=48 << 20),
        cost_estimate=pl.CostEstimate(
            flops=half * 2 * D * FF * 600, bytes_accessed=2 * x.size, transcendentals=0
        ),
    )(seeds, x, share, gate_w, up_w).reshape(experts, slots, FF)


def down_kernel(
    devices, local_count, seeds, act, place, out, lin, made, y, sent, arrived, send_sem, recv_sem
):
    step_now = pl.program_id(0)
    tiles = pl.num_programs(0) - 1
    experts, slots, _ = act.shape
    tok_dev, width = out.shape
    me = lax.axis_index("node") * local_count + lax.axis_index("local")
    halves = DOWN_COLS // COLS
    units = experts * halves
    done = step_now - 1
    slot = lax.rem(step_now, 2)

    def peer(step):
        return lax.rem(me + step, devices)

    def device(index):
        return {"node": index // local_count, "local": lax.rem(index, local_count)}

    barrier = pltpu.get_barrier_semaphore()

    def make(tile, unit):
        expert, half = unit // halves, unit % halves
        base = offset(seeds[expert], salt_down, 0, tile * DOWN_COLS + half * COLS, D)
        hash_rows(made, (unit % 2,), lin, base, FF, D)

    def use(unit):
        expert, half = unit // halves, unit % halves
        part = jnp.dot(act[expert], made[unit % 2], preferred_element_type=jnp.float32)
        y[expert * slots : (expert + 1) * slots, half * COLS : (half + 1) * COLS] = (
            part * SCALE_OUT
        ).astype(jnp.bfloat16)

    def combine():
        sent[slot] = jnp.dot(place[...], y[...], preferred_element_type=jnp.float32).astype(jnp.bfloat16)

    def copy(step, where, column):
        to = peer(step)
        return pltpu.make_async_remote_copy(
            src_ref=sent.at[where, pl.ds(pl.multiple_of(to * tok_dev, tok_dev), tok_dev), :],
            dst_ref=arrived.at[me, :, pl.ds(pl.multiple_of(column * DOWN_COLS, DOWN_COLS), DOWN_COLS)],
            send_sem=send_sem.at[where, to],
            recv_sem=recv_sem.at[me],
            device_id=device(to),
            device_id_type=pl.DeviceIdType.MESH,
        )

    @pl.when(step_now == 0)
    def _():
        @pl.loop(1, devices)
        def _(step):
            pl.semaphore_signal(
                barrier, inc=1, device_id=device(peer(step)), device_id_type=pl.DeviceIdType.MESH
            )

        fill_index(lin, D)
        y[...] = jnp.zeros_like(y)
        make(0, 0)

    @pl.when(step_now == 1)
    def _():
        pl.semaphore_wait(barrier, devices - 1)

    @pl.when(step_now >= 3)
    def _():
        @pl.loop(1, devices)
        def _(step):
            copy(step, slot, done - 2).wait_send()

    @pl.when(step_now < tiles)
    def _():
        combine()
        make(step_now, 1)
        use(0)

    @pl.when(step_now == tiles)
    def _():
        combine()

    @pl.when(step_now >= 1)
    def _():
        @pl.loop(1, devices)
        def _(step):
            copy(step, slot, done).start()

        own = pl.ds(pl.multiple_of(me * tok_dev, tok_dev), tok_dev)
        columns = pl.ds(pl.multiple_of(done * DOWN_COLS, DOWN_COLS), DOWN_COLS)
        arrived[me, :, columns] = sent[slot, own, :]

    @pl.when(step_now < tiles)
    def _():
        for unit in range(1, units):
            make(step_now + (unit + 1) // units, (unit + 1) % units)
            use(unit)

    @pl.when(step_now == tiles)
    def _():
        @pl.loop(1, devices)
        def _(step):
            copy(step, 1 - slot, done - 1).wait_send()
            copy(step, slot, done).wait_send()
            source = peer(step)
            pltpu.make_async_remote_copy(
                src_ref=arrived.at[source],
                dst_ref=arrived.at[source],
                send_sem=send_sem.at[0, source],
                recv_sem=recv_sem.at[source],
                device_id=device(source),
                device_id_type=pl.DeviceIdType.MESH,
            ).wait_recv()

        @pl.loop(0, width // DOWN_COLS)
        def _(part):
            span = pl.ds(pl.multiple_of(part * DOWN_COLS, DOWN_COLS), DOWN_COLS)

            def add(source, total):
                return total + arrived[source, :, span].astype(jnp.float32)

            total = lax.fori_loop(0, devices, add, jnp.zeros((tok_dev, DOWN_COLS), jnp.float32))
            out[:, span] = total.astype(jnp.bfloat16)


def run_down(seeds, act, place, tok_dev, width, devices, local_count):
    experts, slots, _ = act.shape
    tokens = place.shape[0]
    return pl.pallas_call(
        functools.partial(down_kernel, devices, local_count),
        grid=(width // DOWN_COLS + 1,),
        in_specs=[
            pl.BlockSpec(memory_space=pltpu.SMEM),
            pl.BlockSpec(act.shape, lambda t: (0, 0, 0)),
            pl.BlockSpec(place.shape, lambda t: (0, 0)),
        ],
        out_specs=pl.BlockSpec((tok_dev, width), lambda t: (0, 0)),
        out_shape=jax.ShapeDtypeStruct((tok_dev, width), jnp.bfloat16),
        scratch_shapes=[
            pltpu.VMEM((PIECE, COLS), jnp.int32),
            pltpu.VMEM((2, FF, COLS), jnp.bfloat16),
            pltpu.VMEM((experts * slots, DOWN_COLS), jnp.bfloat16),
            pltpu.VMEM((2, tokens, DOWN_COLS), jnp.bfloat16),
            pltpu.VMEM((devices, tok_dev, width), jnp.bfloat16),
            pltpu.SemaphoreType.DMA((2, devices)),
            pltpu.SemaphoreType.DMA((devices,)),
        ],
        compiler_params=pltpu.CompilerParams(
            vmem_limit_bytes=56 << 20, collective_id=0, has_side_effects=True
        ),
        cost_estimate=pl.CostEstimate(
            flops=experts * 2 * width * FF * 600, bytes_accessed=2 * tokens * width, transcendentals=0
        ),
    )(seeds, act, place)


def routing(meta, first_expert, group_size, capacity, tok_dev):
    total = meta.shape[0]
    sources = total // tok_dev
    ids, levels, groups = meta[:, :TOP], meta[:, TOP : 2 * TOP], meta[:, 2 * TOP :]
    in_group = jnp.any((ids // group_size)[:, :, None] == groups[:, None, :], axis=2)
    levels = levels.astype(jnp.float32)
    gate = (
        route_scale * levels * in_group.astype(jnp.float32) / jnp.sum(levels, axis=1, keepdims=True)
    )
    mine = first_expert + jnp.arange(EXP_DEV, dtype=jnp.int32)
    chosen = (ids[:, :, None] == mine) & in_group[:, :, None]
    hit = jnp.any(chosen, axis=1)
    share = jnp.sum(jnp.where(chosen, gate[:, :, None], 0.0), axis=1)
    earlier = jnp.tril(jnp.ones((tok_dev, tok_dev), jnp.bfloat16), -1)
    rank = jnp.einsum(
        "ts,bse->bte",
        earlier,
        hit.astype(jnp.bfloat16).reshape(sources, tok_dev, EXP_DEV),
        preferred_element_type=jnp.float32,
    ).reshape(total, EXP_DEV).astype(jnp.int32)
    source = (jnp.arange(total, dtype=jnp.int32) // tok_dev)[:, None]
    slot = jnp.where(hit & (rank < capacity), source * capacity + rank, -1)
    slots = jnp.arange(sources * capacity, dtype=jnp.int32)
    place = (slot[:, :, None] == slots).astype(jnp.bfloat16).reshape(total, -1)
    pick = slot.T[:, None, :] == slots[None, :, None]
    slot_share = jnp.sum(jnp.where(pick, share.T[:, None, :], 0.0), axis=2, keepdims=True)
    return pick.astype(jnp.bfloat16), place, slot_share


def on_device(tokens, expert_ids, node_groups, gate_levels, expert_seeds):
    tok_dev, width = tokens.shape
    devices_all = lax.axis_size(AXES)
    local_count = lax.axis_size("local")
    experts_total = EXP_DEV * devices_all
    capacity = max(2, tok_dev * TOP // experts_total)
    me = lax.axis_index("node") * local_count + lax.axis_index("local")

    meta = jnp.concatenate([expert_ids, gate_levels, node_groups], axis=1).astype(jnp.bfloat16)
    meta = jnp.pad(meta, ((0, 0), (0, META - meta.shape[1])))
    every = lax.all_gather(jnp.concatenate([tokens, meta], axis=1), AXES, axis=0, tiled=True)
    gate_w, up_w = make_weights(expert_seeds)
    pick, place, share = routing(
        every[:, width : width + 2 * TOP + node_groups.shape[1]].astype(jnp.int32),
        me * EXP_DEV,
        EXP_DEV * local_count,
        capacity,
        tok_dev,
    )

    slots = pick.shape[1]
    x = jnp.dot(
        pick.reshape(EXP_DEV * slots, -1), every, preferred_element_type=jnp.float32
    ).astype(jnp.bfloat16).reshape(EXP_DEV, slots, -1)
    act = run_up(expert_seeds, x, share, gate_w, up_w)
    return run_down(expert_seeds, act, place, tok_dev, width, devices_all, local_count)


def solution(mesh):
    rows = P(("rep", "node", "local"), None)
    return jax.shard_map(
        on_device,
        mesh=mesh,
        in_specs=(rows, rows, rows, rows, P(AXES)),
        out_specs=rows,
        check_vma=False,
    )
```

```python
import functools
import math

import jax
import jax.numpy as jnp
from jax import lax
from jax.experimental import pallas as pl
from jax.experimental.pallas import tpu as pltpu
from jax.sharding import PartitionSpec as P

D = 7168
FF = 1024
TOP = 8
EXP_DEV = 4
AXES = ("node", "local")

route_scale = 2.5
salt_gate = 1013904223
salt_up = 1664525
salt_down = 22695477
INDEX_MUL = 747796405
SEED_MUL = 1103515245
SCALE_IN = math.sqrt(3.0 / D) / 8388608.0
SCALE_OUT = math.sqrt(3.0 / FF) / 8388608.0

ROWS = 512
COLS = 256
PIECE = 64
DOWN_COLS = 512
AHEAD = 2
META = 128


def as_int32(value):
    return jnp.int32((value + 2**31) % 2**32 - 2**31)


def centred(hashed):
    hashed = hashed ^ (hashed >> 15)
    hashed = hashed * jnp.int32(277803737)
    hashed = hashed ^ (hashed >> 13)
    hashed = hashed * jnp.int32(668265263)
    hashed = hashed ^ (hashed >> 16)
    sixteen = (hashed & jnp.int32(65535 << 8)).astype(jnp.float32)
    return (sixteen - 32767.5 * 256.0).astype(jnp.bfloat16)


def fill_index(lin, columns):
    row = lax.broadcasted_iota(jnp.int32, lin.shape, 0)
    col = lax.broadcasted_iota(jnp.int32, lin.shape, 1)
    lin[...] = (row * columns + col) * as_int32(INDEX_MUL)


def hash_rows(out, where, lin, base, rows, columns):
    for piece in range(0, rows, PIECE):
        start = base + as_int32(piece * columns * INDEX_MUL)
        out[(*where, slice(piece, piece + PIECE), slice(None))] = centred(lin[...] + start)


def offset(seed, salt, row, col, columns):
    return (row * columns + col) * as_int32(INDEX_MUL) + seed * as_int32(SEED_MUL) + jnp.int32(salt)


def make_kernel(seeds, gate_out, up_out, lin):
    expert = pl.program_id(0)
    tile = pl.program_id(1)

    @pl.when((expert == 0) & (tile == 0))
    def _():
        fill_index(lin, FF)

    seed = seeds[EXP_DEV - AHEAD + expert]

    @pl.loop(0, D // ROWS)
    def _(step):
        rows = pl.ds(pl.multiple_of(step * ROWS, ROWS), ROWS)
        for salt, out in ((salt_gate, gate_out), (salt_up, up_out)):
            base = offset(seed, salt, step * ROWS, tile * COLS, FF)
            hash_rows(out.at[0, rows, :], (), lin, base, ROWS, FF)


def make_weights(seeds):
    spec = pl.BlockSpec((1, D, COLS), lambda e, t: (e, 0, t))
    return pl.pallas_call(
        make_kernel,
        grid=(AHEAD, FF // COLS),
        in_specs=[pl.BlockSpec(memory_space=pltpu.SMEM)],
        out_specs=[spec, spec],
        out_shape=[jax.ShapeDtypeStruct((AHEAD, D, FF), jnp.bfloat16)] * 2,
        scratch_shapes=[pltpu.VMEM((PIECE, COLS), jnp.int32)],
        compiler_params=pltpu.CompilerParams(vmem_limit_bytes=48 << 20),
        cost_estimate=pl.CostEstimate(
            flops=AHEAD * 2 * D * FF * 600, bytes_accessed=AHEAD * 4 * D * FF, transcendentals=0
        ),
    )(seeds)


def activation(gate_part, up_part, share):
    g = gate_part * SCALE_IN
    return (g / (1.0 + jnp.exp(-g)) * (up_part * SCALE_IN) * share).astype(jnp.bfloat16)


def up_kernel(seeds, x, share, gate_w, up_w, act, lin, made, acc):
    expert = pl.program_id(0)
    tile = pl.program_id(1)

    @pl.when((expert == 0) & (tile == 0))
    def _():
        fill_index(lin, FF)

    acc[...] = jnp.zeros_like(acc)
    seed = seeds[expert]

    def make(step, slot):
        for which, salt in enumerate((salt_gate, salt_up)):
            base = offset(seed, salt, step * ROWS, tile * COLS, FF)
            hash_rows(made, (slot, which), lin, base, ROWS, FF)

    def use(step, slot):
        rows = pl.ds(pl.multiple_of(step * ROWS, ROWS), ROWS)
        hashed_x, ready_x = x[0, 0, :, rows], x[1, 0, :, rows]
        for which, ready in enumerate((gate_w, up_w)):
            acc[2 + which] += jnp.dot(ready_x, ready[0, rows, :], preferred_element_type=jnp.float32)
            acc[which] += jnp.dot(hashed_x, made[slot, which], preferred_element_type=jnp.float32)

    steps = D // ROWS
    make(0, 0)

    @pl.loop(0, steps // 2 - 1)
    def _(pair):
        make(2 * pair + 1, 1)
        use(2 * pair, 0)
        make(2 * pair + 2, 0)
        use(2 * pair + 1, 1)

    make(steps - 1, 1)
    use(steps - 2, 0)
    use(steps - 1, 1)

    act[0, 0] = activation(acc[0], acc[1], share[0, 0])
    act[1, 0] = activation(acc[2], acc[3], share[1, 0])


def run_up(seeds, x, share, gate_w, up_w):
    experts, slots, _ = x.shape
    half = experts - AHEAD
    x = x.reshape(2, half, slots, -1)
    share = share.reshape(2, half, slots, 1)
    weights = pl.BlockSpec((1, D, COLS), lambda e, t: (e, 0, t))
    return pl.pallas_call(
        up_kernel,
        grid=(half, FF // COLS),
        in_specs=[
            pl.BlockSpec(memory_space=pltpu.SMEM),
            pl.BlockSpec((2, 1, slots, D), lambda e, t: (0, e, 0, 0)),
            pl.BlockSpec((2, 1, slots, 1), lambda e, t: (0, e, 0, 0)),
            weights,
            weights,
        ],
        out_specs=pl.BlockSpec((2, 1, slots, COLS), lambda e, t: (0, e, 0, t)),
        out_shape=jax.ShapeDtypeStruct((2, half, slots, FF), jnp.bfloat16),
        scratch_shapes=[
            pltpu.VMEM((PIECE, COLS), jnp.int32),
            pltpu.VMEM((2, 2, ROWS, COLS), jnp.bfloat16),
            pltpu.VMEM((4, slots, COLS), jnp.float32),
        ],
        compiler_params=pltpu.CompilerParams(vmem_limit_bytes=48 << 20),
        cost_estimate=pl.CostEstimate(
            flops=half * 2 * D * FF * 600, bytes_accessed=2 * x.size, transcendentals=0
        ),
    )(seeds, x, share, gate_w, up_w).reshape(experts, slots, FF)


def pairs_along_node(nodes, locals_):
    return locals_ < nodes


def down_kernel(
    nodes, locals_, seeds, act, place, out,
    lin, made, y, sent, paired, pushed, arrived,
    pair_send, pair_recv, push_send, push_recv,
):
    step_now = pl.program_id(0)
    tiles = pl.num_programs(0) - 2
    experts, slots, _ = act.shape
    tok_dev, width = out.shape
    node, local = lax.axis_index("node"), lax.axis_index("local")
    half_devices = nodes * locals_ // 2
    by_node = pairs_along_node(nodes, locals_)
    side = lax.rem(node, 2) if by_node else lax.rem(local, 2)
    me = node // 2 * locals_ + local if by_node else node * (locals_ // 2) + local // 2
    halves = DOWN_COLS // COLS
    units = experts * halves
    done = step_now - 1
    onward = step_now - 2
    slot = lax.rem(step_now, 2)

    def device(index):
        if by_node:
            return {"node": index // locals_ * 2 + side, "local": lax.rem(index, locals_)}
        per_node = locals_ // 2
        return {"node": index // per_node, "local": lax.rem(index, per_node) * 2 + side}

    def peer(step):
        return lax.rem(me + step, half_devices)

    if by_node:
        sibling = {"node": node + 1 - 2 * side, "local": local}
    else:
        sibling = {"node": node, "local": local + 1 - 2 * side}

    barrier = pltpu.get_barrier_semaphore()

    def make(tile, unit):
        expert, half = unit // halves, unit % halves
        base = offset(seeds[expert], salt_down, 0, tile * DOWN_COLS + half * COLS, D)
        hash_rows(made, (unit % 2,), lin, base, FF, D)

    def use(unit):
        expert, half = unit // halves, unit % halves
        part = jnp.dot(act[expert], made[unit % 2], preferred_element_type=jnp.float32)
        y[expert * slots : (expert + 1) * slots, half * COLS : (half + 1) * COLS] = (
            part * SCALE_OUT
        ).astype(jnp.bfloat16)

    def combine():
        sent[slot] = jnp.dot(place[...], y[...], preferred_element_type=jnp.float32).astype(jnp.bfloat16)

    def block(index):
        return pl.ds(pl.multiple_of(index * tok_dev, tok_dev), tok_dev)

    def columns(tile):
        return pl.ds(pl.multiple_of(tile * DOWN_COLS, DOWN_COLS), DOWN_COLS)

    def pair_copy(where, tile):
        rows = half_devices * tok_dev
        return pltpu.make_async_remote_copy(
            src_ref=sent.at[where, pl.ds(pl.multiple_of((1 - side) * rows, rows), rows), :],
            dst_ref=paired.at[:, columns(tile)],
            send_sem=pair_send.at[where],
            recv_sem=pair_recv.at[tile],
            device_id=sibling,
            device_id_type=pl.DeviceIdType.MESH,
        )

    def push(step, where, tile):
        to = peer(step)
        return pltpu.make_async_remote_copy(
            src_ref=pushed.at[where, block(to), :],
            dst_ref=arrived.at[me, :, columns(tile)],
            send_sem=push_send.at[where, to],
            recv_sem=push_recv.at[me],
            device_id=device(to),
            device_id_type=pl.DeviceIdType.MESH,
        )

    def greet(other):
        pl.semaphore_signal(barrier, inc=1, device_id=other, device_id_type=pl.DeviceIdType.MESH)

    @pl.when(step_now == 0)
    def _():
        greet(sibling)

        @pl.loop(1, half_devices)
        def _(step):
            greet(device(peer(step)))

        fill_index(lin, D)
        y[...] = jnp.zeros_like(y)
        make(0, 0)

    @pl.when(step_now == 1)
    def _():
        pl.semaphore_wait(barrier, half_devices)

    @pl.when(step_now >= 4)
    def _():
        @pl.loop(1, half_devices)
        def _(step):
            push(step, slot, onward - 2).wait_send()

    @pl.when(step_now >= 2)
    def _():
        pair_copy(1 - slot, onward).wait_recv()

        @pl.loop(0, half_devices)
        def _(index):
            mine = sent[1 - slot, block(side * half_devices + index), :].astype(jnp.float32)
            theirs = paired[block(index), columns(onward)].astype(jnp.float32)
            pushed[slot, block(index), :] = (mine + theirs).astype(jnp.bfloat16)

        @pl.loop(1, half_devices)
        def _(step):
            push(step, slot, onward).start()

        arrived[me, :, columns(onward)] = pushed[slot, block(me), :]

    @pl.when((step_now >= 3) & (step_now <= tiles))
    def _():
        pair_copy(slot, done - 2).wait_send()

    @pl.when(step_now < tiles)
    def _():
        combine()
        make(step_now, 1)
        use(0)

    @pl.when(step_now == tiles)
    def _():
        combine()

    @pl.when((step_now >= 1) & (step_now <= tiles))
    def _():
        pair_copy(slot, done).start()

    @pl.when(step_now < tiles)
    def _():
        for unit in range(1, units):
            make(step_now + (unit + 1) // units, (unit + 1) % units)
            use(unit)

    @pl.when(step_now == tiles + 1)
    def _():
        pair_copy(slot, tiles - 2).wait_send()
        pair_copy(1 - slot, tiles - 1).wait_send()

        @pl.loop(1, half_devices)
        def _(step):
            push(step, 1 - slot, onward - 1).wait_send()
            push(step, slot, onward).wait_send()
            source = peer(step)
            pltpu.make_async_remote_copy(
                src_ref=arrived.at[source],
                dst_ref=arrived.at[source],
                send_sem=push_send.at[0, source],
                recv_sem=push_recv.at[source],
                device_id=device(source),
                device_id_type=pl.DeviceIdType.MESH,
            ).wait_recv()

        @pl.loop(0, width // DOWN_COLS)
        def _(part):
            def add(source, total):
                return total + arrived[source, :, columns(part)].astype(jnp.float32)

            total = lax.fori_loop(0, half_devices, add, jnp.zeros((tok_dev, DOWN_COLS), jnp.float32))
            out[:, columns(part)] = total.astype(jnp.bfloat16)


def run_down(seeds, act, place, tok_dev, width, nodes, locals_):
    experts, slots, _ = act.shape
    half_devices = nodes * locals_ // 2
    tiles = width // DOWN_COLS
    tokens = place.shape[0]
    return pl.pallas_call(
        functools.partial(down_kernel, nodes, locals_),
        grid=(tiles + 2,),
        in_specs=[
            pl.BlockSpec(memory_space=pltpu.SMEM),
            pl.BlockSpec(act.shape, lambda t: (0, 0, 0)),
            pl.BlockSpec(place.shape, lambda t: (0, 0)),
        ],
        out_specs=pl.BlockSpec((tok_dev, width), lambda t: (0, 0)),
        out_shape=jax.ShapeDtypeStruct((tok_dev, width), jnp.bfloat16),
        scratch_shapes=[
            pltpu.VMEM((PIECE, COLS), jnp.int32),
            pltpu.VMEM((2, FF, COLS), jnp.bfloat16),
            pltpu.VMEM((experts * slots, DOWN_COLS), jnp.bfloat16),
            pltpu.VMEM((2, tokens, DOWN_COLS), jnp.bfloat16),
            pltpu.VMEM((tokens // 2, width), jnp.bfloat16),
            pltpu.VMEM((2, tokens // 2, DOWN_COLS), jnp.bfloat16),
            pltpu.VMEM((half_devices, tok_dev, width), jnp.bfloat16),
            pltpu.SemaphoreType.DMA((2,)),
            pltpu.SemaphoreType.DMA((tiles,)),
            pltpu.SemaphoreType.DMA((2, half_devices)),
            pltpu.SemaphoreType.DMA((half_devices,)),
        ],
        compiler_params=pltpu.CompilerParams(
            vmem_limit_bytes=56 << 20, collective_id=0, has_side_effects=True
        ),
        cost_estimate=pl.CostEstimate(
            flops=experts * 2 * width * FF * 600, bytes_accessed=2 * tokens * width, transcendentals=0
        ),
    )(seeds, act, place)


def routing(meta, first_expert, group_size, capacity, tok_dev):
    total = meta.shape[0]
    sources = total // tok_dev
    ids, levels, groups = meta[:, :TOP], meta[:, TOP : 2 * TOP], meta[:, 2 * TOP :]
    in_group = jnp.any((ids // group_size)[:, :, None] == groups[:, None, :], axis=2)
    levels = levels.astype(jnp.float32)
    gate = (
        route_scale * levels * in_group.astype(jnp.float32) / jnp.sum(levels, axis=1, keepdims=True)
    )
    mine = first_expert + jnp.arange(EXP_DEV, dtype=jnp.int32)
    chosen = (ids[:, :, None] == mine) & in_group[:, :, None]
    hit = jnp.any(chosen, axis=1)
    share = jnp.sum(jnp.where(chosen, gate[:, :, None], 0.0), axis=1)
    earlier = jnp.tril(jnp.ones((tok_dev, tok_dev), jnp.bfloat16), -1)
    rank = jnp.einsum(
        "ts,bse->bte",
        earlier,
        hit.astype(jnp.bfloat16).reshape(sources, tok_dev, EXP_DEV),
        preferred_element_type=jnp.float32,
    ).reshape(total, EXP_DEV).astype(jnp.int32)
    source = (jnp.arange(total, dtype=jnp.int32) // tok_dev)[:, None]
    slot = jnp.where(hit & (rank < capacity), source * capacity + rank, -1)
    slots = jnp.arange(sources * capacity, dtype=jnp.int32)
    place = (slot[:, :, None] == slots).astype(jnp.bfloat16).reshape(total, -1)
    pick = slot.T[:, None, :] == slots[None, :, None]
    slot_share = jnp.sum(jnp.where(pick, share.T[:, None, :], 0.0), axis=2, keepdims=True)
    return pick.astype(jnp.bfloat16), place, slot_share


def on_device(tokens, expert_ids, node_groups, gate_levels, expert_seeds):
    tok_dev, width = tokens.shape
    devices_all = lax.axis_size(AXES)
    local_count = lax.axis_size("local")
    experts_total = EXP_DEV * devices_all
    capacity = max(2, tok_dev * TOP // experts_total)
    me = lax.axis_index("node") * local_count + lax.axis_index("local")

    meta = jnp.concatenate([expert_ids, gate_levels, node_groups], axis=1).astype(jnp.bfloat16)
    meta = jnp.pad(meta, ((0, 0), (0, META - meta.shape[1])))
    every = lax.all_gather(jnp.concatenate([tokens, meta], axis=1), AXES, axis=0, tiled=True)
    gate_w, up_w = make_weights(expert_seeds)
    pick, place, share = routing(
        every[:, width : width + 2 * TOP + node_groups.shape[1]].astype(jnp.int32),
        me * EXP_DEV,
        EXP_DEV * local_count,
        capacity,
        tok_dev,
    )

    slots = pick.shape[1]
    x = jnp.dot(
        pick.reshape(EXP_DEV * slots, -1), every, preferred_element_type=jnp.float32
    ).astype(jnp.bfloat16).reshape(EXP_DEV, slots, -1)
    act = run_up(expert_seeds, x, share, gate_w, up_w)
    nodes = devices_all // local_count
    if pairs_along_node(nodes, local_count):
        place = place.reshape(nodes // 2, 2, local_count, tok_dev, -1).transpose(1, 0, 2, 3, 4)
    else:
        place = place.reshape(nodes, local_count // 2, 2, tok_dev, -1).transpose(2, 0, 1, 3, 4)
    place = place.reshape(devices_all * tok_dev, -1)
    return run_down(expert_seeds, act, place, tok_dev, width, nodes, local_count)


def solution(mesh):
    rows = P(("rep", "node", "local"), None)
    return jax.shard_map(
        on_device,
        mesh=mesh,
        in_specs=(rows, rows, rows, rows, P(AXES)),
        out_specs=rows,
        check_vma=False,
    )
```

```python
import functools
import math

import jax
import jax.numpy as jnp
from jax import lax
from jax.experimental import pallas as pl
from jax.experimental.pallas import tpu as pltpu
from jax.sharding import PartitionSpec as P

D = 7168
FF = 1024
TOP = 8
EXP_DEV = 4
AXES = ("node", "local")

route_scale = 2.5
salt_gate = 1013904223
salt_up = 1664525
salt_down = 22695477
INDEX_MUL = 747796405
SEED_MUL = 1103515245
SCALE_IN = math.sqrt(3.0 / D) / 8388608.0
SCALE_OUT = math.sqrt(3.0 / FF) / 8388608.0

ROWS = 512
COLS = 256
PIECE = 64
DOWN_COLS = 512
AHEAD = 2
META = 128


def as_int32(value):
    return jnp.int32((value + 2**31) % 2**32 - 2**31)


def centred(hashed):
    hashed = hashed ^ (hashed >> 15)
    hashed = hashed * jnp.int32(277803737)
    hashed = hashed ^ (hashed >> 13)
    hashed = hashed * jnp.int32(668265263)
    hashed = hashed ^ (hashed >> 16)
    sixteen = (hashed & jnp.int32(65535 << 8)).astype(jnp.float32)
    return (sixteen - 32767.5 * 256.0).astype(jnp.bfloat16)


def fill_index(lin, columns):
    row = lax.broadcasted_iota(jnp.int32, lin.shape, 0)
    col = lax.broadcasted_iota(jnp.int32, lin.shape, 1)
    lin[...] = (row * columns + col) * as_int32(INDEX_MUL)


def hash_rows(out, where, lin, base, rows, columns):
    for piece in range(0, rows, PIECE):
        start = base + as_int32(piece * columns * INDEX_MUL)
        out[(*where, slice(piece, piece + PIECE), slice(None))] = centred(lin[...] + start)


def offset(seed, salt, row, col, columns):
    return (row * columns + col) * as_int32(INDEX_MUL) + seed * as_int32(SEED_MUL) + jnp.int32(salt)


def make_kernel(seeds, gate_out, up_out, lin):
    expert = pl.program_id(0)
    tile = pl.program_id(1)

    @pl.when((expert == 0) & (tile == 0))
    def _():
        fill_index(lin, FF)

    seed = seeds[EXP_DEV - AHEAD + expert]

    @pl.loop(0, D // ROWS)
    def _(step):
        rows = pl.ds(pl.multiple_of(step * ROWS, ROWS), ROWS)
        for salt, out in ((salt_gate, gate_out), (salt_up, up_out)):
            base = offset(seed, salt, step * ROWS, tile * COLS, FF)
            hash_rows(out.at[0, rows, :], (), lin, base, ROWS, FF)


def make_weights(seeds):
    spec = pl.BlockSpec((1, D, COLS), lambda e, t: (e, 0, t))
    return pl.pallas_call(
        make_kernel,
        grid=(AHEAD, FF // COLS),
        in_specs=[pl.BlockSpec(memory_space=pltpu.SMEM)],
        out_specs=[spec, spec],
        out_shape=[jax.ShapeDtypeStruct((AHEAD, D, FF), jnp.bfloat16)] * 2,
        scratch_shapes=[pltpu.VMEM((PIECE, COLS), jnp.int32)],
        compiler_params=pltpu.CompilerParams(vmem_limit_bytes=48 << 20),
        cost_estimate=pl.CostEstimate(
            flops=AHEAD * 2 * D * FF * 600, bytes_accessed=AHEAD * 4 * D * FF, transcendentals=0
        ),
    )(seeds)


def activation(gate_part, up_part, share):
    g = gate_part * SCALE_IN
    return (g / (1.0 + jnp.exp(-g)) * (up_part * SCALE_IN) * share).astype(jnp.bfloat16)


def up_kernel(first, seeds, x, share, gate_w, up_w, act, lin, made, acc):
    expert = pl.program_id(0)
    tile = pl.program_id(1)

    @pl.when((expert == 0) & (tile == 0))
    def _():
        fill_index(lin, FF)

    acc[...] = jnp.zeros_like(acc)
    seed = seeds[expert]

    def make(step, slot):
        for which, salt in enumerate((salt_gate, salt_up)):
            base = offset(seed, salt, step * ROWS, (first + tile) * COLS, FF)
            hash_rows(made, (slot, which), lin, base, ROWS, FF)

    def use(step, slot):
        rows = pl.ds(pl.multiple_of(step * ROWS, ROWS), ROWS)
        hashed_x, ready_x = x[0, 0, :, rows], x[1, 0, :, rows]
        for which, ready in enumerate((gate_w, up_w)):
            acc[2 + which] += jnp.dot(ready_x, ready[0, rows, :], preferred_element_type=jnp.float32)
            acc[which] += jnp.dot(hashed_x, made[slot, which], preferred_element_type=jnp.float32)

    steps = D // ROWS
    make(0, 0)

    @pl.loop(0, steps // 2 - 1)
    def _(pair):
        make(2 * pair + 1, 1)
        use(2 * pair, 0)
        make(2 * pair + 2, 0)
        use(2 * pair + 1, 1)

    make(steps - 1, 1)
    use(steps - 2, 0)
    use(steps - 1, 1)

    act[0, 0] = activation(acc[0], acc[1], share[0, 0])
    act[1, 0] = activation(acc[2], acc[3], share[1, 0])


def run_up(seeds, x, share, gate_w, up_w, first, count):
    experts, slots, _ = x.shape
    half = experts - AHEAD
    x = x.reshape(2, half, slots, -1)
    share = share.reshape(2, half, slots, 1)
    weights = pl.BlockSpec((1, D, COLS), lambda e, t: (e, 0, first + t))
    return pl.pallas_call(
        functools.partial(up_kernel, first),
        grid=(half, count),
        in_specs=[
            pl.BlockSpec(memory_space=pltpu.SMEM),
            pl.BlockSpec((2, 1, slots, D), lambda e, t: (0, e, 0, 0)),
            pl.BlockSpec((2, 1, slots, 1), lambda e, t: (0, e, 0, 0)),
            weights,
            weights,
        ],
        out_specs=pl.BlockSpec((2, 1, slots, COLS), lambda e, t: (0, e, 0, t)),
        out_shape=jax.ShapeDtypeStruct((2, half, slots, count * COLS), jnp.bfloat16),
        scratch_shapes=[
            pltpu.VMEM((PIECE, COLS), jnp.int32),
            pltpu.VMEM((2, 2, ROWS, COLS), jnp.bfloat16),
            pltpu.VMEM((4, slots, COLS), jnp.float32),
        ],
        compiler_params=pltpu.CompilerParams(vmem_limit_bytes=48 << 20),
        cost_estimate=pl.CostEstimate(
            flops=half * 2 * D * count * COLS * 600, bytes_accessed=2 * x.size, transcendentals=0
        ),
    )(seeds, x, share, gate_w, up_w).reshape(experts, slots, count * COLS)


def pairs_along_node(nodes, locals_):
    return locals_ < nodes


def down_kernel(
    nodes, locals_, seeds, act_main, act_rest, other_main, other_rest, place, out,
    lin, made, y, sent, paired, pushed, arrived,
    pair_send, pair_recv, push_send, push_recv,
):
    step_now = pl.program_id(0)
    tiles = pl.num_programs(0) - 2
    experts, slots, main = act_main.shape
    tok_dev, width = out.shape
    part_width = width // 2
    rep = lax.axis_index("rep")
    zside = lax.rem(rep, 2)
    partner = rep + 1 - 2 * zside
    node, local = lax.axis_index("node"), lax.axis_index("local")
    half_devices = nodes * locals_ // 2
    by_node = pairs_along_node(nodes, locals_)
    side = lax.rem(node, 2) if by_node else lax.rem(local, 2)
    me = node // 2 * locals_ + local if by_node else node * (locals_ // 2) + local // 2
    halves = DOWN_COLS // COLS
    units = experts * halves
    done = step_now - 1
    onward = step_now - 2
    slot = lax.rem(step_now, 2)

    def device(index):
        if by_node:
            return {"node": index // locals_ * 2 + side, "local": lax.rem(index, locals_)}
        per_node = locals_ // 2
        return {"node": index // per_node, "local": lax.rem(index, per_node) * 2 + side}

    def target(which, index):
        return {"rep": partner if which else rep, **device(index)}

    def peer(step):
        return lax.rem(me + step, half_devices)

    def each_target(act_on):
        @pl.loop(0, half_devices)
        def _(step):
            act_on(1, step)

        @pl.loop(1, half_devices)
        def _(step):
            act_on(0, step)

    if by_node:
        sibling = {"rep": rep, "node": node + 1 - 2 * side, "local": local}
    else:
        sibling = {"rep": rep, "node": node, "local": local + 1 - 2 * side}

    barrier = pltpu.get_barrier_semaphore()

    def make(tile, unit):
        expert, half = unit // halves, unit % halves
        base = offset(
            seeds[expert], salt_down, 0, zside * part_width + tile * DOWN_COLS + half * COLS, D
        )
        hash_rows(made, (unit % 2,), lin, base, FF, D)

    def use(unit):
        expert, half = unit // halves, unit % halves
        rows_main = jnp.concatenate([act_main[expert], other_main[expert]], axis=0)
        rows_rest = jnp.concatenate([act_rest[expert], other_rest[expert]], axis=0)
        part = jnp.dot(rows_main, made[unit % 2, :main], preferred_element_type=jnp.float32)
        part += jnp.dot(rows_rest, made[unit % 2, main:], preferred_element_type=jnp.float32)
        part = (part * SCALE_OUT).astype(jnp.bfloat16)
        for which in range(2):
            y[
                which, expert * slots : (expert + 1) * slots, half * COLS : (half + 1) * COLS
            ] = part[which * slots : (which + 1) * slots]

    rows = half_devices * tok_dev

    def combine():
        for which in range(2):
            for part in range(2):
                sent[slot, part, which] = jnp.dot(
                    place[which, part * rows : (part + 1) * rows],
                    y[which],
                    preferred_element_type=jnp.float32,
                ).astype(jnp.bfloat16)

    def block(index):
        return pl.ds(pl.multiple_of(index * tok_dev, tok_dev), tok_dev)

    def columns(tile):
        return pl.ds(pl.multiple_of(tile * DOWN_COLS, DOWN_COLS), DOWN_COLS)

    def pair_copy(where, tile):
        return pltpu.make_async_remote_copy(
            src_ref=sent.at[where, 1 - side],
            dst_ref=paired.at[:, :, columns(tile)],
            send_sem=pair_send.at[where],
            recv_sem=pair_recv.at[tile],
            device_id=sibling,
            device_id_type=pl.DeviceIdType.MESH,
        )

    def push(which, step, where, tile):
        to = peer(step)
        return pltpu.make_async_remote_copy(
            src_ref=pushed.at[where, which, block(to), :],
            dst_ref=arrived.at[which, me, :, columns(tile)],
            send_sem=push_send.at[where, which, to],
            recv_sem=push_recv.at[which, me],
            device_id=target(which, to),
            device_id_type=pl.DeviceIdType.MESH,
        )

    def greet(other):
        pl.semaphore_signal(barrier, inc=1, device_id=other, device_id_type=pl.DeviceIdType.MESH)

    @pl.when(step_now == 0)
    def _():
        greet(sibling)

        each_target(lambda which, step: greet(target(which, peer(step))))

        fill_index(lin, D)
        y[...] = jnp.zeros_like(y)
        make(0, 0)

    @pl.when(step_now == 1)
    def _():
        pl.semaphore_wait(barrier, 2 * half_devices)

    @pl.when(step_now >= 4)
    def _():
        each_target(lambda which, step: push(which, step, slot, onward - 2).wait_send())

    @pl.when(step_now >= 2)
    def _():
        pair_copy(1 - slot, onward).wait_recv()

        @pl.loop(0, half_devices)
        def _(index):
            for which in range(2):
                mine = sent[1 - slot, side, which, block(index), :].astype(jnp.float32)
                theirs = paired[which, block(index), columns(onward)].astype(jnp.float32)
                pushed[slot, which, block(index), :] = (mine + theirs).astype(jnp.bfloat16)

        each_target(lambda which, step: push(which, step, slot, onward).start())
        arrived[0, me, :, columns(onward)] = pushed[slot, 0, block(me), :]

    @pl.when((step_now >= 3) & (step_now <= tiles))
    def _():
        pair_copy(slot, done - 2).wait_send()

    @pl.when(step_now < tiles)
    def _():
        combine()
        make(step_now, 1)
        use(0)

    @pl.when(step_now == tiles)
    def _():
        combine()

    @pl.when((step_now >= 1) & (step_now <= tiles))
    def _():
        pair_copy(slot, done).start()

    @pl.when(step_now < tiles)
    def _():
        for unit in range(1, units):
            make(step_now + (unit + 1) // units, (unit + 1) % units)
            use(unit)

    @pl.when(step_now == tiles + 1)
    def _():
        pair_copy(slot, tiles - 2).wait_send()
        pair_copy(1 - slot, tiles - 1).wait_send()

        def finish(which, step):
            push(which, step, 1 - slot, onward - 1).wait_send()
            push(which, step, slot, onward).wait_send()
            source = peer(step)
            pltpu.make_async_remote_copy(
                src_ref=arrived.at[which, source],
                dst_ref=arrived.at[which, source],
                send_sem=push_send.at[0, which, source],
                recv_sem=push_recv.at[which, source],
                device_id=target(which, source),
                device_id_type=pl.DeviceIdType.MESH,
            ).wait_recv()

        each_target(finish)

        for which in range(2):
            start = (zside if which == 0 else 1 - zside) * part_width

            @pl.loop(0, part_width // DOWN_COLS)
            def _(part):
                def add(source, total):
                    return total + arrived[which, source, :, columns(part)].astype(jnp.float32)

                total = lax.fori_loop(
                    0, half_devices, add, jnp.zeros((tok_dev, DOWN_COLS), jnp.float32)
                )
                span = pl.ds(pl.multiple_of(start + part * DOWN_COLS, DOWN_COLS), DOWN_COLS)
                out[:, span] = total.astype(jnp.bfloat16)


def run_down(seeds, acts, place, tok_dev, width, nodes, locals_):
    experts, slots, _ = acts[0].shape
    half_devices = nodes * locals_ // 2
    tiles = width // 2 // DOWN_COLS
    tokens = place.shape[1]
    return pl.pallas_call(
        functools.partial(down_kernel, nodes, locals_),
        grid=(tiles + 2,),
        in_specs=[
            pl.BlockSpec(memory_space=pltpu.SMEM),
            *[pl.BlockSpec(act.shape, lambda t: (0, 0, 0)) for act in acts],
            pl.BlockSpec(place.shape, lambda t: (0, 0, 0)),
        ],
        out_specs=pl.BlockSpec((tok_dev, width), lambda t: (0, 0)),
        out_shape=jax.ShapeDtypeStruct((tok_dev, width), jnp.bfloat16),
        scratch_shapes=[
            pltpu.VMEM((PIECE, COLS), jnp.int32),
            pltpu.VMEM((2, FF, COLS), jnp.bfloat16),
            pltpu.VMEM((2, experts * slots, DOWN_COLS), jnp.bfloat16),
            pltpu.VMEM((2, 2, 2, tokens // 2, DOWN_COLS), jnp.bfloat16),
            pltpu.VMEM((2, tokens // 2, width // 2), jnp.bfloat16),
            pltpu.VMEM((2, 2, tokens // 2, DOWN_COLS), jnp.bfloat16),
            pltpu.VMEM((2, half_devices, tok_dev, width // 2), jnp.bfloat16),
            pltpu.SemaphoreType.DMA((2,)),
            pltpu.SemaphoreType.DMA((tiles,)),
            pltpu.SemaphoreType.DMA((2, 2, half_devices)),
            pltpu.SemaphoreType.DMA((2, half_devices)),
        ],
        compiler_params=pltpu.CompilerParams(
            vmem_limit_bytes=60 << 20, collective_id=0, has_side_effects=True
        ),
        cost_estimate=pl.CostEstimate(
            flops=experts * width * FF * 600, bytes_accessed=2 * tokens * width, transcendentals=0
        ),
    )(seeds, *acts, place)


def routing(meta, first_expert, group_size, capacity, tok_dev):
    total = meta.shape[0]
    sources = total // tok_dev
    ids, levels, groups = meta[:, :TOP], meta[:, TOP : 2 * TOP], meta[:, 2 * TOP :]
    in_group = jnp.any((ids // group_size)[:, :, None] == groups[:, None, :], axis=2)
    levels = levels.astype(jnp.float32)
    gate = (
        route_scale * levels * in_group.astype(jnp.float32) / jnp.sum(levels, axis=1, keepdims=True)
    )
    mine = first_expert + jnp.arange(EXP_DEV, dtype=jnp.int32)
    chosen = (ids[:, :, None] == mine) & in_group[:, :, None]
    hit = jnp.any(chosen, axis=1)
    share = jnp.sum(jnp.where(chosen, gate[:, :, None], 0.0), axis=1)
    earlier = jnp.tril(jnp.ones((tok_dev, tok_dev), jnp.bfloat16), -1)
    rank = jnp.einsum(
        "ts,bse->bte",
        earlier,
        hit.astype(jnp.bfloat16).reshape(sources, tok_dev, EXP_DEV),
        preferred_element_type=jnp.float32,
    ).reshape(total, EXP_DEV).astype(jnp.int32)
    source = (jnp.arange(total, dtype=jnp.int32) // tok_dev)[:, None]
    slot = jnp.where(hit & (rank < capacity), source * capacity + rank, -1)
    slots = jnp.arange(sources * capacity, dtype=jnp.int32)
    place = (slot[:, :, None] == slots).astype(jnp.bfloat16).reshape(total, -1)
    pick = slot.T[:, None, :] == slots[None, :, None]
    slot_share = jnp.sum(jnp.where(pick, share.T[:, None, :], 0.0), axis=2, keepdims=True)
    return pick.astype(jnp.bfloat16), place, slot_share


def on_device(tokens, expert_ids, node_groups, gate_levels, expert_seeds):
    tok_dev, width = tokens.shape
    devices_all = lax.axis_size(AXES)
    local_count = lax.axis_size("local")
    experts_total = EXP_DEV * devices_all
    capacity = max(2, tok_dev * TOP // experts_total)
    me = lax.axis_index("node") * local_count + lax.axis_index("local")

    meta = jnp.concatenate([expert_ids, gate_levels, node_groups], axis=1).astype(jnp.bfloat16)
    meta = jnp.pad(meta, ((0, 0), (0, META - meta.shape[1])))
    every = lax.all_gather(jnp.concatenate([tokens, meta], axis=1), AXES, axis=0, tiled=True)
    gate_w, up_w = make_weights(expert_seeds)
    pick, place, share = routing(
        every[:, width : width + 2 * TOP + node_groups.shape[1]].astype(jnp.int32),
        me * EXP_DEV,
        EXP_DEV * local_count,
        capacity,
        tok_dev,
    )

    slots = pick.shape[1]
    x = jnp.dot(
        pick.reshape(EXP_DEV * slots, -1), every, preferred_element_type=jnp.float32
    ).astype(jnp.bfloat16).reshape(EXP_DEV, slots, -1)
    swap = [(rep, rep ^ 1) for rep in range(lax.axis_size("rep"))]
    tiles = FF // COLS
    act_main = run_up(expert_seeds, x, share, gate_w, up_w, 0, tiles - 1)
    other_main = lax.ppermute(act_main, "rep", swap)
    act_rest = run_up(expert_seeds, x, share, gate_w, up_w, tiles - 1, 1)
    other_rest = lax.ppermute(act_rest, "rep", swap)
    nodes = devices_all // local_count
    if pairs_along_node(nodes, local_count):
        place = place.reshape(nodes // 2, 2, local_count, tok_dev, -1).transpose(1, 0, 2, 3, 4)
    else:
        place = place.reshape(nodes, local_count // 2, 2, tok_dev, -1).transpose(2, 0, 1, 3, 4)
    place = place.reshape(devices_all * tok_dev, -1)
    place = jnp.stack([place, lax.ppermute(place, "rep", swap)])
    acts = (act_main, act_rest, other_main, other_rest)
    return run_down(expert_seeds, acts, place, tok_dev, width, nodes, local_count)


def solution(mesh):
    rows = P(("rep", "node", "local"), None)
    return jax.shard_map(
        on_device,
        mesh=mesh,
        in_specs=(rows, rows, rows, rows, P(AXES)),
        out_specs=rows,
        check_vma=False,
    )
```

```python
import functools
import math

import jax
import jax.numpy as jnp
from jax import lax
from jax.experimental import pallas as pl
from jax.experimental.pallas import tpu as pltpu
from jax.sharding import PartitionSpec as P

D = 7168
FF = 1024
TOP = 8
EXP_DEV = 4
AXES = ("node", "local")

route_scale = 2.5
salt_gate = 1013904223
salt_up = 1664525
salt_down = 22695477
INDEX_MUL = 747796405
SEED_MUL = 1103515245
SCALE_IN = math.sqrt(3.0 / D) / 8388608.0
SCALE_OUT = math.sqrt(3.0 / FF) / 8388608.0

ROWS = 512
COLS = 256
PIECE = 64
DOWN_COLS = 256
AHEAD = 2
META = 128


def as_int32(value):
    return jnp.int32((value + 2**31) % 2**32 - 2**31)


def centred(hashed):
    hashed = hashed ^ (hashed >> 15)
    hashed = hashed * jnp.int32(277803737)
    hashed = hashed ^ (hashed >> 13)
    hashed = hashed * jnp.int32(668265263)
    hashed = hashed ^ (hashed >> 16)
    sixteen = (hashed & jnp.int32(65535 << 8)).astype(jnp.float32)
    return (sixteen - 32767.5 * 256.0).astype(jnp.bfloat16)


def fill_index(lin, columns):
    row = lax.broadcasted_iota(jnp.int32, lin.shape, 0)
    col = lax.broadcasted_iota(jnp.int32, lin.shape, 1)
    lin[...] = (row * columns + col) * as_int32(INDEX_MUL)


def hash_rows(out, where, lin, base, rows, columns):
    for piece in range(0, rows, PIECE):
        start = base + as_int32(piece * columns * INDEX_MUL)
        out[(*where, slice(piece, piece + PIECE), slice(None))] = centred(lin[...] + start)


def offset(seed, salt, row, col, columns):
    return (row * columns + col) * as_int32(INDEX_MUL) + seed * as_int32(SEED_MUL) + jnp.int32(salt)


def make_kernel(seeds, gate_out, up_out, lin):
    expert = pl.program_id(0)
    tile = pl.program_id(1)

    @pl.when((expert == 0) & (tile == 0))
    def _():
        fill_index(lin, FF)

    seed = seeds[EXP_DEV - AHEAD + expert]

    @pl.loop(0, D // ROWS)
    def _(step):
        rows = pl.ds(pl.multiple_of(step * ROWS, ROWS), ROWS)
        for salt, out in ((salt_gate, gate_out), (salt_up, up_out)):
            base = offset(seed, salt, step * ROWS, tile * COLS, FF)
            hash_rows(out.at[0, rows, :], (), lin, base, ROWS, FF)


def make_weights(seeds):
    spec = pl.BlockSpec((1, D, COLS), lambda e, t: (e, 0, t))
    return pl.pallas_call(
        make_kernel,
        grid=(AHEAD, FF // COLS),
        in_specs=[pl.BlockSpec(memory_space=pltpu.SMEM)],
        out_specs=[spec, spec],
        out_shape=[jax.ShapeDtypeStruct((AHEAD, D, FF), jnp.bfloat16)] * 2,
        scratch_shapes=[pltpu.VMEM((PIECE, COLS), jnp.int32)],
        compiler_params=pltpu.CompilerParams(vmem_limit_bytes=48 << 20),
        cost_estimate=pl.CostEstimate(
            flops=AHEAD * 2 * D * FF * 600, bytes_accessed=AHEAD * 4 * D * FF, transcendentals=0
        ),
    )(seeds)


def activation(gate_part, up_part, share):
    g = gate_part * SCALE_IN
    return (g / (1.0 + jnp.exp(-g)) * (up_part * SCALE_IN) * share).astype(jnp.bfloat16)


def up_kernel(first, seeds, x, share, gate_w, up_w, act, lin, made, acc):
    expert = pl.program_id(0)
    tile = pl.program_id(1)

    @pl.when((expert == 0) & (tile == 0))
    def _():
        fill_index(lin, FF)

    acc[...] = jnp.zeros_like(acc)
    seed = seeds[expert]

    def make(step, slot):
        for which, salt in enumerate((salt_gate, salt_up)):
            base = offset(seed, salt, step * ROWS, (first + tile) * COLS, FF)
            hash_rows(made, (slot, which), lin, base, ROWS, FF)

    def use(step, slot):
        rows = pl.ds(pl.multiple_of(step * ROWS, ROWS), ROWS)
        hashed_x, ready_x = x[0, 0, :, rows], x[1, 0, :, rows]
        for which, ready in enumerate((gate_w, up_w)):
            acc[2 + which] += jnp.dot(ready_x, ready[0, rows, :], preferred_element_type=jnp.float32)
            acc[which] += jnp.dot(hashed_x, made[slot, which], preferred_element_type=jnp.float32)

    steps = D // ROWS
    make(0, 0)

    @pl.loop(0, steps // 2 - 1)
    def _(pair):
        make(2 * pair + 1, 1)
        use(2 * pair, 0)
        make(2 * pair + 2, 0)
        use(2 * pair + 1, 1)

    make(steps - 1, 1)
    use(steps - 2, 0)
    use(steps - 1, 1)

    act[0, 0] = activation(acc[0], acc[1], share[0, 0])
    act[1, 0] = activation(acc[2], acc[3], share[1, 0])


def run_up(seeds, x, share, gate_w, up_w, first, count):
    experts, slots, _ = x.shape
    half = experts - AHEAD
    x = x.reshape(2, half, slots, -1)
    share = share.reshape(2, half, slots, 1)
    weights = pl.BlockSpec((1, D, COLS), lambda e, t: (e, 0, first + t))
    return pl.pallas_call(
        functools.partial(up_kernel, first),
        grid=(half, count),
        in_specs=[
            pl.BlockSpec(memory_space=pltpu.SMEM),
            pl.BlockSpec((2, 1, slots, D), lambda e, t: (0, e, 0, 0)),
            pl.BlockSpec((2, 1, slots, 1), lambda e, t: (0, e, 0, 0)),
            weights,
            weights,
        ],
        out_specs=pl.BlockSpec((2, 1, slots, COLS), lambda e, t: (0, e, 0, t)),
        out_shape=jax.ShapeDtypeStruct((2, half, slots, count * COLS), jnp.bfloat16),
        scratch_shapes=[
            pltpu.VMEM((PIECE, COLS), jnp.int32),
            pltpu.VMEM((2, 2, ROWS, COLS), jnp.bfloat16),
            pltpu.VMEM((4, slots, COLS), jnp.float32),
        ],
        compiler_params=pltpu.CompilerParams(vmem_limit_bytes=48 << 20),
        cost_estimate=pl.CostEstimate(
            flops=half * 2 * D * count * COLS * 600, bytes_accessed=2 * x.size, transcendentals=0
        ),
    )(seeds, x, share, gate_w, up_w).reshape(experts, slots, count * COLS)


def pairs_along_node(nodes, locals_):
    return locals_ < nodes


def down_kernel(
    nodes, locals_, seeds, act_main, act_rest, other_main, other_rest, place, out,
    lin, made, y, sent, paired, pushed, arrived,
    pair_send, pair_recv, push_send, push_recv,
):
    step_now = pl.program_id(0)
    tiles = pl.num_programs(0) - 1
    experts, slots, main = act_main.shape
    tok_dev, width = out.shape
    part_width = width // 2
    rep = lax.axis_index("rep")
    zside = lax.rem(rep, 2)
    partner = rep + 1 - 2 * zside
    node, local = lax.axis_index("node"), lax.axis_index("local")
    half_devices = nodes * locals_ // 2
    by_node = pairs_along_node(nodes, locals_)
    side = lax.rem(node, 2) if by_node else lax.rem(local, 2)
    me = node // 2 * locals_ + local if by_node else node * (locals_ // 2) + local // 2
    halves = DOWN_COLS // COLS
    units = experts * halves
    done = step_now - 1
    slot = lax.rem(step_now, 2)

    def device(index):
        if by_node:
            return {"node": index // locals_ * 2 + side, "local": lax.rem(index, locals_)}
        per_node = locals_ // 2
        return {"node": index // per_node, "local": lax.rem(index, per_node) * 2 + side}

    def target(which, index):
        return {"rep": partner if which else rep, **device(index)}

    def peer(step):
        return lax.rem(me + step, half_devices)

    def each_target(act_on):
        @pl.loop(0, half_devices)
        def _(step):
            act_on(1, step)

        @pl.loop(1, half_devices)
        def _(step):
            act_on(0, step)

    if by_node:
        sibling = {"rep": rep, "node": node + 1 - 2 * side, "local": local}
    else:
        sibling = {"rep": rep, "node": node, "local": local + 1 - 2 * side}

    barrier = pltpu.get_barrier_semaphore()

    def make(tile, unit):
        expert, half = unit // halves, unit % halves
        base = offset(
            seeds[expert], salt_down, 0, zside * part_width + tile * DOWN_COLS + half * COLS, D
        )
        hash_rows(made, (unit % 2,), lin, base, FF, D)

    def use(unit):
        expert, half = unit // halves, unit % halves
        rows_main = jnp.concatenate([act_main[expert], other_main[expert]], axis=0)
        rows_rest = jnp.concatenate([act_rest[expert], other_rest[expert]], axis=0)
        part = jnp.dot(rows_main, made[unit % 2, :main], preferred_element_type=jnp.float32)
        part += jnp.dot(rows_rest, made[unit % 2, main:], preferred_element_type=jnp.float32)
        part = (part * SCALE_OUT).astype(jnp.bfloat16)
        for which in range(2):
            y[
                which, expert * slots : (expert + 1) * slots, half * COLS : (half + 1) * COLS
            ] = part[which * slots : (which + 1) * slots]

    rows = half_devices * tok_dev

    def combine():
        for which in range(2):
            for part in range(2):
                sent[slot, part, which] = jnp.dot(
                    place[which, part * rows : (part + 1) * rows],
                    y[which],
                    preferred_element_type=jnp.float32,
                ).astype(jnp.bfloat16)

    def block(index):
        return pl.ds(pl.multiple_of(index * tok_dev, tok_dev), tok_dev)

    def columns(tile):
        return pl.ds(pl.multiple_of(tile * DOWN_COLS, DOWN_COLS), DOWN_COLS)

    def pair_copy(where, tile):
        return pltpu.make_async_remote_copy(
            src_ref=sent.at[where, 1 - side],
            dst_ref=paired.at[:, :, columns(tile)],
            send_sem=pair_send.at[where],
            recv_sem=pair_recv.at[tile],
            device_id=sibling,
            device_id_type=pl.DeviceIdType.MESH,
        )

    def push(which, step, where, tile):
        to = peer(step)
        return pltpu.make_async_remote_copy(
            src_ref=pushed.at[where, which, block(to), :],
            dst_ref=arrived.at[which, me, :, columns(tile)],
            send_sem=push_send.at[where, which, to],
            recv_sem=push_recv.at[which, me],
            device_id=target(which, to),
            device_id_type=pl.DeviceIdType.MESH,
        )

    def greet(other):
        pl.semaphore_signal(barrier, inc=1, device_id=other, device_id_type=pl.DeviceIdType.MESH)

    @pl.when(step_now == 0)
    def _():
        greet(sibling)

        each_target(lambda which, step: greet(target(which, peer(step))))

        fill_index(lin, D)
        y[...] = jnp.zeros_like(y)
        make(0, 0)

    @pl.when(step_now == 1)
    def _():
        pl.semaphore_wait(barrier, 2 * half_devices)

    @pl.when(step_now >= 3)
    def _():
        pair_copy(slot, done - 2).wait_send()

    @pl.when(step_now < tiles)
    def _():
        combine()
        make(step_now, 1)
        use(0)

    @pl.when(step_now == tiles)
    def _():
        combine()

    @pl.when(step_now >= 1)
    def _():
        pair_copy(slot, done).start()

    def run_units(first, last):
        @pl.when(step_now < tiles)
        def _():
            for unit in range(first, last):
                make(step_now + (unit + 1) // units, (unit + 1) % units)
                use(unit)

    run_units(1, units - 1)

    @pl.when(step_now >= 3)
    def _():
        each_target(lambda which, step: push(which, step, slot, done - 2).wait_send())

    @pl.when(step_now >= 1)
    def _():
        pair_copy(slot, done).wait_recv()

        @pl.loop(0, half_devices)
        def _(index):
            for which in range(2):
                mine = sent[slot, side, which, block(index), :].astype(jnp.float32)
                theirs = paired[which, block(index), columns(done)].astype(jnp.float32)
                pushed[slot, which, block(index), :] = (mine + theirs).astype(jnp.bfloat16)

        each_target(lambda which, step: push(which, step, slot, done).start())
        arrived[0, me, :, columns(done)] = pushed[slot, 0, block(me), :]

    run_units(units - 1, units)

    @pl.when(step_now == tiles)
    def _():
        pair_copy(1 - slot, tiles - 2).wait_send()
        pair_copy(slot, tiles - 1).wait_send()

        def finish(which, step):
            push(which, step, 1 - slot, done - 1).wait_send()
            push(which, step, slot, done).wait_send()
            source = peer(step)
            pltpu.make_async_remote_copy(
                src_ref=arrived.at[which, source],
                dst_ref=arrived.at[which, source],
                send_sem=push_send.at[0, which, source],
                recv_sem=push_recv.at[which, source],
                device_id=target(which, source),
                device_id_type=pl.DeviceIdType.MESH,
            ).wait_recv()

        each_target(finish)

        for which in range(2):
            start = (zside if which == 0 else 1 - zside) * part_width

            @pl.loop(0, part_width // DOWN_COLS)
            def _(part):
                def add(source, total):
                    return total + arrived[which, source, :, columns(part)].astype(jnp.float32)

                total = lax.fori_loop(
                    0, half_devices, add, jnp.zeros((tok_dev, DOWN_COLS), jnp.float32)
                )
                span = pl.ds(pl.multiple_of(start + part * DOWN_COLS, DOWN_COLS), DOWN_COLS)
                out[:, span] = total.astype(jnp.bfloat16)


def run_down(seeds, acts, place, tok_dev, width, nodes, locals_):
    experts, slots, _ = acts[0].shape
    half_devices = nodes * locals_ // 2
    tiles = width // 2 // DOWN_COLS
    tokens = place.shape[1]
    return pl.pallas_call(
        functools.partial(down_kernel, nodes, locals_),
        grid=(tiles + 1,),
        in_specs=[
            pl.BlockSpec(memory_space=pltpu.SMEM),
            *[pl.BlockSpec(act.shape, lambda t: (0, 0, 0)) for act in acts],
            pl.BlockSpec(place.shape, lambda t: (0, 0, 0)),
        ],
        out_specs=pl.BlockSpec((tok_dev, width), lambda t: (0, 0)),
        out_shape=jax.ShapeDtypeStruct((tok_dev, width), jnp.bfloat16),
        scratch_shapes=[
            pltpu.VMEM((PIECE, COLS), jnp.int32),
            pltpu.VMEM((2, FF, COLS), jnp.bfloat16),
            pltpu.VMEM((2, experts * slots, DOWN_COLS), jnp.bfloat16),
            pltpu.VMEM((2, 2, 2, tokens // 2, DOWN_COLS), jnp.bfloat16),
            pltpu.VMEM((2, tokens // 2, width // 2), jnp.bfloat16),
            pltpu.VMEM((2, 2, tokens // 2, DOWN_COLS), jnp.bfloat16),
            pltpu.VMEM((2, half_devices, tok_dev, width // 2), jnp.bfloat16),
            pltpu.SemaphoreType.DMA((2,)),
            pltpu.SemaphoreType.DMA((tiles,)),
            pltpu.SemaphoreType.DMA((2, 2, half_devices)),
            pltpu.SemaphoreType.DMA((2, half_devices)),
        ],
        compiler_params=pltpu.CompilerParams(
            vmem_limit_bytes=60 << 20, collective_id=0, has_side_effects=True
        ),
        cost_estimate=pl.CostEstimate(
            flops=experts * width * FF * 600, bytes_accessed=2 * tokens * width, transcendentals=0
        ),
    )(seeds, *acts, place)


def routing(meta, first_expert, group_size, capacity, tok_dev):
    total = meta.shape[0]
    sources = total // tok_dev
    ids, levels, groups = meta[:, :TOP], meta[:, TOP : 2 * TOP], meta[:, 2 * TOP :]
    in_group = jnp.any((ids // group_size)[:, :, None] == groups[:, None, :], axis=2)
    levels = levels.astype(jnp.float32)
    gate = (
        route_scale * levels * in_group.astype(jnp.float32) / jnp.sum(levels, axis=1, keepdims=True)
    )
    mine = first_expert + jnp.arange(EXP_DEV, dtype=jnp.int32)
    chosen = (ids[:, :, None] == mine) & in_group[:, :, None]
    hit = jnp.any(chosen, axis=1)
    share = jnp.sum(jnp.where(chosen, gate[:, :, None], 0.0), axis=1)
    earlier = jnp.tril(jnp.ones((tok_dev, tok_dev), jnp.bfloat16), -1)
    rank = jnp.einsum(
        "ts,bse->bte",
        earlier,
        hit.astype(jnp.bfloat16).reshape(sources, tok_dev, EXP_DEV),
        preferred_element_type=jnp.float32,
    ).reshape(total, EXP_DEV).astype(jnp.int32)
    source = (jnp.arange(total, dtype=jnp.int32) // tok_dev)[:, None]
    slot = jnp.where(hit & (rank < capacity), source * capacity + rank, -1)
    slots = jnp.arange(sources * capacity, dtype=jnp.int32)
    pick = slot.T[:, None, :] == slots[None, :, None]
    slot_share = jnp.sum(jnp.where(pick, share.T[:, None, :], 0.0), axis=2, keepdims=True)
    return pick.astype(jnp.bfloat16), slot, slot_share


def on_device(tokens, expert_ids, node_groups, gate_levels, expert_seeds):
    tok_dev, width = tokens.shape
    devices_all = lax.axis_size(AXES)
    local_count = lax.axis_size("local")
    experts_total = EXP_DEV * devices_all
    capacity = max(2, tok_dev * TOP // experts_total)
    me = lax.axis_index("node") * local_count + lax.axis_index("local")

    meta = jnp.concatenate([expert_ids, gate_levels, node_groups], axis=1).astype(jnp.bfloat16)
    meta = jnp.pad(meta, ((0, 0), (0, META - meta.shape[1])))
    every = lax.all_gather(jnp.concatenate([tokens, meta], axis=1), AXES, axis=0, tiled=True)
    gate_w, up_w = make_weights(expert_seeds)
    pick, slot, share = routing(
        every[:, width : width + 2 * TOP + node_groups.shape[1]].astype(jnp.int32),
        me * EXP_DEV,
        EXP_DEV * local_count,
        capacity,
        tok_dev,
    )

    swap = [(rep, rep ^ 1) for rep in range(lax.axis_size("rep"))]
    nodes = devices_all // local_count
    if pairs_along_node(nodes, local_count):
        slot = slot.reshape(nodes // 2, 2, local_count, tok_dev, -1).transpose(1, 0, 2, 3, 4)
    else:
        slot = slot.reshape(nodes, local_count // 2, 2, tok_dev, -1).transpose(2, 0, 1, 3, 4)
    slot = slot.reshape(devices_all * tok_dev, -1)
    slot = jnp.stack([slot, lax.ppermute(slot, "rep", swap)])
    place = (slot[..., None] == jnp.arange(pick.shape[1], dtype=jnp.int32)).astype(jnp.bfloat16)
    place = place.reshape(2, devices_all * tok_dev, -1)

    slots = pick.shape[1]
    x = jnp.dot(
        pick.reshape(EXP_DEV * slots, -1), every, preferred_element_type=jnp.float32
    ).astype(jnp.bfloat16).reshape(EXP_DEV, slots, -1)
    tiles = FF // COLS
    act_main = run_up(expert_seeds, x, share, gate_w, up_w, 0, tiles - 1)
    other_main = lax.ppermute(act_main, "rep", swap)
    share, place = lax.optimization_barrier((share, place))
    act_rest = run_up(expert_seeds, x, share, gate_w, up_w, tiles - 1, 1)
    other_rest = lax.ppermute(act_rest, "rep", swap)
    acts = (act_main, act_rest, other_main, other_rest)
    return run_down(expert_seeds, acts, place, tok_dev, width, nodes, local_count)


def solution(mesh):
    rows = P(("rep", "node", "local"), None)
    return jax.shard_map(
        on_device,
        mesh=mesh,
        in_specs=(rows, rows, rows, rows, P(AXES)),
        out_specs=rows,
        check_vma=False,
    )
```

```python
import functools
import math

import jax
import jax.numpy as jnp
from jax import lax
from jax.experimental import pallas as pl
from jax.experimental.pallas import tpu as pltpu
from jax.sharding import PartitionSpec as P

D = 7168
FF = 1024
TOP = 8
EXP_DEV = 4
AXES = ("node", "local")

route_scale = 2.5
salt_gate = 1013904223
salt_up = 1664525
salt_down = 22695477
INDEX_MUL = 747796405
SEED_MUL = 1103515245
SCALE_IN = math.sqrt(3.0 / D) / 8388608.0
SCALE_OUT = math.sqrt(3.0 / FF) / 8388608.0

ROWS = 512
COLS = 256
PIECE = 64
DOWN_COLS = 256
AHEAD = 2
META = 128


def as_int32(value):
    return jnp.int32((value + 2**31) % 2**32 - 2**31)


def centred(hashed):
    hashed = hashed ^ (hashed >> 15)
    hashed = hashed * jnp.int32(277803737)
    hashed = hashed ^ (hashed >> 13)
    hashed = hashed * jnp.int32(668265263)
    hashed = hashed ^ (hashed >> 16)
    sixteen = (hashed & jnp.int32(65535 << 8)).astype(jnp.float32)
    return (sixteen - 32767.5 * 256.0).astype(jnp.bfloat16)


def fill_index(lin, columns):
    row = lax.broadcasted_iota(jnp.int32, lin.shape, 0)
    col = lax.broadcasted_iota(jnp.int32, lin.shape, 1)
    lin[...] = (row * columns + col) * as_int32(INDEX_MUL)


def hash_rows(out, where, lin, base, rows, columns):
    for piece in range(0, rows, PIECE):
        start = base + as_int32(piece * columns * INDEX_MUL)
        out[(*where, slice(piece, piece + PIECE), slice(None))] = centred(lin[...] + start)


def offset(seed, salt, row, col, columns):
    return (row * columns + col) * as_int32(INDEX_MUL) + seed * as_int32(SEED_MUL) + jnp.int32(salt)


def make_kernel(seeds, gate_out, up_out, lin):
    expert = pl.program_id(0)
    tile = pl.program_id(1)

    @pl.when((expert == 0) & (tile == 0))
    def _():
        fill_index(lin, FF)

    seed = seeds[EXP_DEV - AHEAD + expert]

    @pl.loop(0, D // ROWS)
    def _(step):
        rows = pl.ds(pl.multiple_of(step * ROWS, ROWS), ROWS)
        for salt, out in ((salt_gate, gate_out), (salt_up, up_out)):
            base = offset(seed, salt, step * ROWS, tile * COLS, FF)
            hash_rows(out.at[0, rows, :], (), lin, base, ROWS, FF)


def make_weights(seeds):
    spec = pl.BlockSpec((1, D, COLS), lambda e, t: (e, 0, t))
    return pl.pallas_call(
        make_kernel,
        grid=(AHEAD, FF // COLS),
        in_specs=[pl.BlockSpec(memory_space=pltpu.SMEM)],
        out_specs=[spec, spec],
        out_shape=[jax.ShapeDtypeStruct((AHEAD, D, FF), jnp.bfloat16)] * 2,
        scratch_shapes=[pltpu.VMEM((PIECE, COLS), jnp.int32)],
        compiler_params=pltpu.CompilerParams(vmem_limit_bytes=48 << 20),
        cost_estimate=pl.CostEstimate(
            flops=AHEAD * 2 * D * FF * 600, bytes_accessed=AHEAD * 4 * D * FF, transcendentals=0
        ),
    )(seeds)


def activation(gate_part, up_part, share):
    g = gate_part * SCALE_IN
    return (g / (1.0 + jnp.exp(-g)) * (up_part * SCALE_IN) * share).astype(jnp.bfloat16)


def up_kernel(first, seeds, x, share, gate_w, up_w, act, lin, made, acc):
    expert = pl.program_id(0)
    tile = pl.program_id(1)

    @pl.when((expert == 0) & (tile == 0))
    def _():
        fill_index(lin, FF)

    acc[...] = jnp.zeros_like(acc)
    seed = seeds[expert]

    def make(step, slot):
        for which, salt in enumerate((salt_gate, salt_up)):
            base = offset(seed, salt, step * ROWS, (first + tile) * COLS, FF)
            hash_rows(made, (slot, which), lin, base, ROWS, FF)

    def use(step, slot):
        rows = pl.ds(pl.multiple_of(step * ROWS, ROWS), ROWS)
        hashed_x, ready_x = x[0, 0, :, rows], x[1, 0, :, rows]
        for which, ready in enumerate((gate_w, up_w)):
            acc[2 + which] += jnp.dot(ready_x, ready[0, rows, :], preferred_element_type=jnp.float32)
            acc[which] += jnp.dot(hashed_x, made[slot, which], preferred_element_type=jnp.float32)

    steps = D // ROWS
    make(0, 0)

    @pl.loop(0, steps // 2 - 1)
    def _(pair):
        make(2 * pair + 1, 1)
        use(2 * pair, 0)
        make(2 * pair + 2, 0)
        use(2 * pair + 1, 1)

    make(steps - 1, 1)
    use(steps - 2, 0)
    use(steps - 1, 1)

    act[0, 0] = activation(acc[0], acc[1], share[0, 0])
    act[1, 0] = activation(acc[2], acc[3], share[1, 0])


def run_up(seeds, x, share, gate_w, up_w, first, count):
    experts, slots, _ = x.shape
    half = experts - AHEAD
    x = x.reshape(2, half, slots, -1)
    share = share.reshape(2, half, slots, 1)
    weights = pl.BlockSpec((1, D, COLS), lambda e, t: (e, 0, first + t))
    return pl.pallas_call(
        functools.partial(up_kernel, first),
        grid=(half, count),
        in_specs=[
            pl.BlockSpec(memory_space=pltpu.SMEM),
            pl.BlockSpec((2, 1, slots, D), lambda e, t: (0, e, 0, 0)),
            pl.BlockSpec((2, 1, slots, 1), lambda e, t: (0, e, 0, 0)),
            weights,
            weights,
        ],
        out_specs=pl.BlockSpec((2, 1, slots, COLS), lambda e, t: (0, e, 0, t)),
        out_shape=jax.ShapeDtypeStruct((2, half, slots, count * COLS), jnp.bfloat16),
        scratch_shapes=[
            pltpu.VMEM((PIECE, COLS), jnp.int32),
            pltpu.VMEM((2, 2, ROWS, COLS), jnp.bfloat16),
            pltpu.VMEM((4, slots, COLS), jnp.float32),
        ],
        compiler_params=pltpu.CompilerParams(vmem_limit_bytes=48 << 20),
        cost_estimate=pl.CostEstimate(
            flops=half * 2 * D * count * COLS * 600, bytes_accessed=2 * x.size, transcendentals=0
        ),
    )(seeds, x, share, gate_w, up_w).reshape(experts, slots, count * COLS)


def pairs_along_node(nodes, locals_):
    return locals_ < nodes


def down_kernel(
    nodes, locals_, seeds, act_main, act_rest, other_main, other_rest, token_slot, out,
    place, lin, made, y, sent, paired, pushed, arrived,
    pair_send, pair_recv, push_send, push_recv,
):
    step_now = pl.program_id(0)
    tiles = pl.num_programs(0) - 1
    experts, slots, main = act_main.shape
    tok_dev, width = out.shape
    part_width = width // 2
    rep = lax.axis_index("rep")
    zside = lax.rem(rep, 2)
    partner = rep + 1 - 2 * zside
    node, local = lax.axis_index("node"), lax.axis_index("local")
    half_devices = nodes * locals_ // 2
    by_node = pairs_along_node(nodes, locals_)
    side = lax.rem(node, 2) if by_node else lax.rem(local, 2)
    me = node // 2 * locals_ + local if by_node else node * (locals_ // 2) + local // 2
    halves = DOWN_COLS // COLS
    units = experts * halves
    done = step_now - 1
    slot = lax.rem(step_now, 2)

    def device(index):
        if by_node:
            return {"node": index // locals_ * 2 + side, "local": lax.rem(index, locals_)}
        per_node = locals_ // 2
        return {"node": index // per_node, "local": lax.rem(index, per_node) * 2 + side}

    def target(which, index):
        return {"rep": partner if which else rep, **device(index)}

    def peer(step):
        return lax.rem(me + step, half_devices)

    def each_target(act_on):
        @pl.loop(0, half_devices)
        def _(step):
            act_on(1, step)

        @pl.loop(1, half_devices)
        def _(step):
            act_on(0, step)

    if by_node:
        sibling = {"rep": rep, "node": node + 1 - 2 * side, "local": local}
    else:
        sibling = {"rep": rep, "node": node, "local": local + 1 - 2 * side}

    barrier = pltpu.get_barrier_semaphore()

    def make(tile, unit):
        expert, half = unit // halves, unit % halves
        base = offset(
            seeds[expert], salt_down, 0, zside * part_width + tile * DOWN_COLS + half * COLS, D
        )
        hash_rows(made, (unit % 2,), lin, base, FF, D)

    def use(unit):
        expert, half = unit // halves, unit % halves
        rows_main = jnp.concatenate([act_main[expert], other_main[expert]], axis=0)
        rows_rest = jnp.concatenate([act_rest[expert], other_rest[expert]], axis=0)
        part = jnp.dot(rows_main, made[unit % 2, :main], preferred_element_type=jnp.float32)
        part += jnp.dot(rows_rest, made[unit % 2, main:], preferred_element_type=jnp.float32)
        part = (part * SCALE_OUT).astype(jnp.bfloat16)
        for which in range(2):
            y[
                which, expert * slots : (expert + 1) * slots, half * COLS : (half + 1) * COLS
            ] = part[which * slots : (which + 1) * slots]

    rows = half_devices * tok_dev

    def combine():
        for which in range(2):
            for part in range(2):
                sent[slot, part, which] = jnp.dot(
                    place[which, part * rows : (part + 1) * rows],
                    y[which],
                    preferred_element_type=jnp.float32,
                ).astype(jnp.bfloat16)

    def block(index):
        return pl.ds(pl.multiple_of(index * tok_dev, tok_dev), tok_dev)

    def columns(tile):
        return pl.ds(pl.multiple_of(tile * DOWN_COLS, DOWN_COLS), DOWN_COLS)

    def pair_copy(where, tile):
        return pltpu.make_async_remote_copy(
            src_ref=sent.at[where, 1 - side],
            dst_ref=paired.at[:, :, columns(tile)],
            send_sem=pair_send.at[where],
            recv_sem=pair_recv.at[tile],
            device_id=sibling,
            device_id_type=pl.DeviceIdType.MESH,
        )

    def push(which, step, where, tile):
        to = peer(step)
        return pltpu.make_async_remote_copy(
            src_ref=pushed.at[where, which, block(to), :],
            dst_ref=arrived.at[which, me, :, columns(tile)],
            send_sem=push_send.at[where, which, to],
            recv_sem=push_recv.at[which, me],
            device_id=target(which, to),
            device_id_type=pl.DeviceIdType.MESH,
        )

    def greet(other):
        pl.semaphore_signal(barrier, inc=1, device_id=other, device_id_type=pl.DeviceIdType.MESH)

    @pl.when(step_now == 0)
    def _():
        greet(sibling)

        each_target(lambda which, step: greet(target(which, peer(step))))

        fill_index(lin, D)

        @pl.loop(0, place.shape[1] // tok_dev)
        def _(index):
            number = lax.broadcasted_iota(jnp.int32, (tok_dev, slots), 1)
            for which in range(2):
                theirs = token_slot[which, block(index), :]
                for expert in range(experts):
                    hit = theirs[:, expert : expert + 1] == number
                    place[which, block(index), expert * slots : (expert + 1) * slots] = jnp.where(
                        hit, 1.0, 0.0
                    ).astype(jnp.bfloat16)

        y[...] = jnp.zeros_like(y)
        make(0, 0)

    @pl.when(step_now == 1)
    def _():
        pl.semaphore_wait(barrier, 2 * half_devices)

    @pl.when(step_now >= 3)
    def _():
        pair_copy(slot, done - 2).wait_send()

    @pl.when(step_now < tiles)
    def _():
        combine()
        make(step_now, 1)
        use(0)

    @pl.when(step_now == tiles)
    def _():
        combine()

    @pl.when(step_now >= 1)
    def _():
        pair_copy(slot, done).start()

    def run_units(first, last):
        @pl.when(step_now < tiles)
        def _():
            for unit in range(first, last):
                make(step_now + (unit + 1) // units, (unit + 1) % units)
                use(unit)

    run_units(1, units - 1)

    @pl.when(step_now >= 3)
    def _():
        each_target(lambda which, step: push(which, step, slot, done - 2).wait_send())

    @pl.when(step_now >= 1)
    def _():
        pair_copy(slot, done).wait_recv()

        @pl.loop(0, half_devices)
        def _(index):
            for which in range(2):
                mine = sent[slot, side, which, block(index), :].astype(jnp.float32)
                theirs = paired[which, block(index), columns(done)].astype(jnp.float32)
                pushed[slot, which, block(index), :] = (mine + theirs).astype(jnp.bfloat16)

        each_target(lambda which, step: push(which, step, slot, done).start())
        arrived[0, me, :, columns(done)] = pushed[slot, 0, block(me), :]

    run_units(units - 1, units)

    @pl.when(step_now == tiles)
    def _():
        pair_copy(1 - slot, tiles - 2).wait_send()
        pair_copy(slot, tiles - 1).wait_send()

        def finish(which, step):
            push(which, step, 1 - slot, done - 1).wait_send()
            push(which, step, slot, done).wait_send()
            source = peer(step)
            pltpu.make_async_remote_copy(
                src_ref=arrived.at[which, source],
                dst_ref=arrived.at[which, source],
                send_sem=push_send.at[0, which, source],
                recv_sem=push_recv.at[which, source],
                device_id=target(which, source),
                device_id_type=pl.DeviceIdType.MESH,
            ).wait_recv()

        each_target(finish)

        for which in range(2):
            start = (zside if which == 0 else 1 - zside) * part_width

            @pl.loop(0, part_width // DOWN_COLS)
            def _(part):
                def add(source, total):
                    return total + arrived[which, source, :, columns(part)].astype(jnp.float32)

                total = lax.fori_loop(
                    0, half_devices, add, jnp.zeros((tok_dev, DOWN_COLS), jnp.float32)
                )
                span = pl.ds(pl.multiple_of(start + part * DOWN_COLS, DOWN_COLS), DOWN_COLS)
                out[:, span] = total.astype(jnp.bfloat16)


def run_down(seeds, acts, slot, tok_dev, width, nodes, locals_):
    experts, slots, _ = acts[0].shape
    half_devices = nodes * locals_ // 2
    tiles = width // 2 // DOWN_COLS
    tokens = slot.shape[1]
    return pl.pallas_call(
        functools.partial(down_kernel, nodes, locals_),
        grid=(tiles + 1,),
        in_specs=[
            pl.BlockSpec(memory_space=pltpu.SMEM),
            *[pl.BlockSpec(act.shape, lambda t: (0, 0, 0)) for act in acts],
            pl.BlockSpec(slot.shape, lambda t: (0, 0, 0)),
        ],
        out_specs=pl.BlockSpec((tok_dev, width), lambda t: (0, 0)),
        out_shape=jax.ShapeDtypeStruct((tok_dev, width), jnp.bfloat16),
        scratch_shapes=[
            pltpu.VMEM((2, tokens, experts * slots), jnp.bfloat16),
            pltpu.VMEM((PIECE, COLS), jnp.int32),
            pltpu.VMEM((2, FF, COLS), jnp.bfloat16),
            pltpu.VMEM((2, experts * slots, DOWN_COLS), jnp.bfloat16),
            pltpu.VMEM((2, 2, 2, tokens // 2, DOWN_COLS), jnp.bfloat16),
            pltpu.VMEM((2, tokens // 2, width // 2), jnp.bfloat16),
            pltpu.VMEM((2, 2, tokens // 2, DOWN_COLS), jnp.bfloat16),
            pltpu.VMEM((2, half_devices, tok_dev, width // 2), jnp.bfloat16),
            pltpu.SemaphoreType.DMA((2,)),
            pltpu.SemaphoreType.DMA((tiles,)),
            pltpu.SemaphoreType.DMA((2, 2, half_devices)),
            pltpu.SemaphoreType.DMA((2, half_devices)),
        ],
        compiler_params=pltpu.CompilerParams(
            vmem_limit_bytes=60 << 20, collective_id=0, has_side_effects=True
        ),
        cost_estimate=pl.CostEstimate(
            flops=experts * width * FF * 600, bytes_accessed=2 * tokens * width, transcendentals=0
        ),
    )(seeds, *acts, slot)


def routing(meta, first_expert, group_size, capacity, tok_dev):
    total = meta.shape[0]
    sources = total // tok_dev
    ids, levels, groups = meta[:, :TOP], meta[:, TOP : 2 * TOP], meta[:, 2 * TOP :]
    in_group = jnp.any((ids // group_size)[:, :, None] == groups[:, None, :], axis=2)
    levels = levels.astype(jnp.float32)
    gate = (
        route_scale * levels * in_group.astype(jnp.float32) / jnp.sum(levels, axis=1, keepdims=True)
    )
    mine = first_expert + jnp.arange(EXP_DEV, dtype=jnp.int32)
    chosen = (ids[:, :, None] == mine) & in_group[:, :, None]
    hit = jnp.any(chosen, axis=1)
    share = jnp.sum(jnp.where(chosen, gate[:, :, None], 0.0), axis=1)
    earlier = jnp.tril(jnp.ones((tok_dev, tok_dev), jnp.bfloat16), -1)
    rank = jnp.einsum(
        "ts,bse->bte",
        earlier,
        hit.astype(jnp.bfloat16).reshape(sources, tok_dev, EXP_DEV),
        preferred_element_type=jnp.float32,
    ).reshape(total, EXP_DEV).astype(jnp.int32)
    source = (jnp.arange(total, dtype=jnp.int32) // tok_dev)[:, None]
    slot = jnp.where(hit & (rank < capacity), source * capacity + rank, -1)
    slots = jnp.arange(sources * capacity, dtype=jnp.int32)
    pick = slot.T[:, None, :] == slots[None, :, None]
    slot_share = jnp.sum(jnp.where(pick, share.T[:, None, :], 0.0), axis=2, keepdims=True)
    return pick.astype(jnp.bfloat16), slot, slot_share


def on_device(tokens, expert_ids, node_groups, gate_levels, expert_seeds):
    tok_dev, width = tokens.shape
    devices_all = lax.axis_size(AXES)
    local_count = lax.axis_size("local")
    experts_total = EXP_DEV * devices_all
    capacity = max(2, tok_dev * TOP // experts_total)
    me = lax.axis_index("node") * local_count + lax.axis_index("local")

    meta = jnp.concatenate([expert_ids, gate_levels, node_groups], axis=1).astype(jnp.bfloat16)
    meta = jnp.pad(meta, ((0, 0), (0, META - meta.shape[1])))
    every = lax.all_gather(jnp.concatenate([tokens, meta], axis=1), AXES, axis=0, tiled=True)
    gate_w, up_w = make_weights(expert_seeds)
    pick, slot, share = routing(
        every[:, width : width + 2 * TOP + node_groups.shape[1]].astype(jnp.int32),
        me * EXP_DEV,
        EXP_DEV * local_count,
        capacity,
        tok_dev,
    )

    swap = [(rep, rep ^ 1) for rep in range(lax.axis_size("rep"))]
    nodes = devices_all // local_count
    if pairs_along_node(nodes, local_count):
        slot = slot.reshape(nodes // 2, 2, local_count, tok_dev, -1).transpose(1, 0, 2, 3, 4)
    else:
        slot = slot.reshape(nodes, local_count // 2, 2, tok_dev, -1).transpose(2, 0, 1, 3, 4)
    slot = slot.reshape(devices_all * tok_dev, -1)
    slot = jnp.stack([slot, lax.ppermute(slot, "rep", swap)])

    slots = pick.shape[1]
    x = jnp.dot(
        pick.reshape(EXP_DEV * slots, -1), every, preferred_element_type=jnp.float32
    ).astype(jnp.bfloat16).reshape(EXP_DEV, slots, -1)
    tiles = FF // COLS
    act_main = run_up(expert_seeds, x, share, gate_w, up_w, 0, tiles - 1)
    other_main = lax.ppermute(act_main, "rep", swap)
    act_rest = run_up(expert_seeds, x, share, gate_w, up_w, tiles - 1, 1)
    other_rest = lax.ppermute(act_rest, "rep", swap)
    acts = (act_main, act_rest, other_main, other_rest)
    return run_down(expert_seeds, acts, slot, tok_dev, width, nodes, local_count)


def solution(mesh):
    rows = P(("rep", "node", "local"), None)
    return jax.shard_map(
        on_device,
        mesh=mesh,
        in_specs=(rows, rows, rows, rows, P(AXES)),
        out_specs=rows,
        check_vma=False,
    )
```
